32 devices in a mesh: runs: 2 (over y), tm: 4 (over z), pix: 4 (over x, core).
Axes of the slice: x: 2, y: 2, z: 4, core: 2. Of those that a mesh axis runs over, the one named last changes fastest.
Arguments:
- frames: bfloat16 [448, 32768], P(('runs', 'tm'), 'pix'), parts along dimension 0, may hold values from 0.049804688 to 20
- labels: int32 [32768], P('pix'), may hold values from -1 to 127, as said below
Outputs:
- two_time: float32 [256, 224, 168], P(('runs', 'pix'), 'tm'), parts along dimension 0
The draws below stay inside these ranges and needn't reach their ends.
There are 2 independent parts, one for each index of `runs`. The reference program is written for one: setup_inputs(seed, part) draws one part's arguments, and reference() takes and returns one part's arrays. A program takes and returns all parts, laid end to end along the dimension named above; an argument that names none is the same for every part. Nothing has to cross between parts.
Inputs may be any that keep to these rules, and one draw needn't show every extreme that they name: `labels`: within the block of 8192 pixels of each pixel group, pixel j lies on cycle j // 64 or is masked (-1); the first pixel of every cycle's slot in every group is unmasked.
All inputs are finite; a program needn't handle non-finite values.
Results may differ from the reference program's by a relative error of at most 0.0003.
Values may be sent and summed in bfloat16 or wider, within the bound.
No kernel may reach another device: no remote copies, remote signals or barrier semaphores. Data moves between devices by JAX's collectives and lax.ppermute only.
A program may use at most 64 MiB of HBM per device.

```python
import math
import jax
import jax.numpy as jnp
from jax import lax

F_DEV = 56
CYCLES = 128
CYCLE_CAP = 64
FRAMES = 224
PIXELS = 32768
N_TM = 4
N_PIX = 4


def draw_labels(key, part):
    key = jax.random.fold_in(key, 7)
    position = jnp.arange(PIXELS, dtype=jnp.int32)
    cycle_of = position // CYCLE_CAP % CYCLES
    leading = position % CYCLE_CAP == 0
    coin = jax.random.randint(key, (PIXELS,), 0, 4)
    return jnp.where((coin > 0) | leading, cycle_of, -1).astype(jnp.int32)


def steps_of(stream_key, extent, split, low, largest):
    factor_of, own = 1.0, jax.random.fold_in(stream_key, 6)
    for dim, shards_of in split:
        draws = jnp.exp(jax.random.uniform(jax.random.fold_in(own, dim), (shards_of,), jnp.float32, low / len(split), largest / len(split)))
        factor_of = factor_of * jnp.repeat(draws, extent[dim] // shards_of).reshape([-1 if axis == dim else 1 for axis in range(len(extent))])
    return factor_of


def setup_inputs(seed: int = 0, part: int = 0) -> dict:
    streams_of = jax.random.split(jax.random.key(seed), 3)
    part_splits = jax.random.split(jax.random.fold_in(streams_of[2], part), 3)
    return {
        "frames": jnp.clip(jnp.exp(math.log(20.0) - 5.9953784 * jax.random.uniform(part_splits[0], (FRAMES, PIXELS), jnp.float32) ** steps_of(part_splits[0], (FRAMES, PIXELS), ((0, 4), (1, 4)), -0.2, 0.2)), 0.049804688, 20.0).astype(jnp.bfloat16),
        "labels": draw_labels(jax.random.fold_in(streams_of[2], 71), part),
    }


def reference(frames, labels):
    live_mask = labels >= 0
    masked = frames * live_mask.astype(jnp.bfloat16)[None, :]
    grouped = masked.reshape(FRAMES, N_PIX, CYCLES, CYCLE_CAP)
    live_grouped = live_mask.reshape(N_PIX, CYCLES, CYCLE_CAP).astype(jnp.float32)
    counts = jnp.sum(live_grouped, axis=(0, 2))
    slot_total = N_TM // 2 + 1
    slot_index = (jnp.arange(N_TM, dtype=jnp.int32)[:, None] + jnp.arange(slot_total, dtype=jnp.int32)[None, :]) % N_TM
    block_rows = jnp.arange(N_TM, dtype=jnp.int32)[:, None]

    def one_cycle(cycle):
        cycle_data = lax.dynamic_index_in_dim(grouped, cycle, axis=2, keepdims=False)
        cycle_data = cycle_data.reshape(FRAMES, N_PIX * CYCLE_CAP)
        gram_full = jnp.dot(cycle_data, cycle_data.T, preferred_element_type=jnp.float32)
        cycle_sums = jnp.sum(cycle_data.astype(jnp.float32), axis=1)
        cycle_count = counts[cycle]
        cycle_means = cycle_sums / cycle_count
        correlation = gram_full / ((cycle_count * cycle_means[:, None]) * cycle_means[None, :])
        tiled = correlation.reshape(N_TM, F_DEV, N_TM, F_DEV).transpose(0, 2, 1, 3)
        chosen = tiled[block_rows, slot_index]
        return chosen.transpose(0, 2, 1, 3).reshape(FRAMES, slot_total * F_DEV)

    return lax.map(one_cycle, jnp.arange(CYCLES, dtype=jnp.int32))
```

```python
import functools

import jax
import jax.numpy as jnp
from jax import lax
from jax.experimental import pallas as pl
from jax.experimental.pallas import tpu as pltpu
from jax.sharding import PartitionSpec as P

CYCLES = 128
CYCLE_CAP = 64
LANES = 128
VMEM_LIMIT = 48 * 2**20


def from_behind(shard, axis, by):
    size = lax.axis_size(axis)
    return lax.ppermute(shard, axis, [(i, (i + by) % size) for i in range(size)])


def swap(shard, axis, by):
    size = lax.axis_size(axis)
    return lax.ppermute(shard, axis, [(i, i ^ by) for i in range(size)])


def ring(frames, labels):
    groups = lax.axis_size("pix")
    loop_size = lax.axis_size("tm")
    local_cycles = CYCLES // groups
    slot_total = loop_size // 2 + 1
    frame_rows = frames.shape[0]
    live_row = (labels >= 0).astype(jnp.bfloat16)[None, :]
    masked = frames * live_row
    own_block, live_owned = (
        lax.all_to_all(masked, "pix", split_axis=1, concat_axis=1, tiled=True),
        lax.all_to_all(live_row, "pix", split_axis=1, concat_axis=1, tiled=True),
    )

    def split_cycles(values):
        return values.reshape(values.shape[:-1] + (groups, local_cycles, CYCLE_CAP))

    counts = jnp.sum(split_cycles(live_owned).astype(jnp.float32), axis=(0, 1, 3))
    own_split = split_cycles(own_block)
    own_means = jnp.sum(own_split, axis=(1, 3), dtype=jnp.float32) / counts

    def make_tiles(blocks):
        block_split = split_cycles(blocks)
        block_means = jnp.sum(block_split, axis=(2, 4), dtype=jnp.float32) / counts
        gram_tiles = jnp.einsum(
            "tgqc,nsgqc->qtns", own_split, block_split, preferred_element_type=jnp.float32
        )
        denominator = (
            counts[:, None, None, None]
            * own_means.T[:, :, None, None]
            * jnp.transpose(block_means, (2, 0, 1))[:, None, :, :]
        )
        return (gram_tiles / denominator).reshape(
            local_cycles, frame_rows, blocks.shape[0] * frame_rows
        )

    filled = jnp.zeros((local_cycles, frame_rows, slot_total * frame_rows), jnp.float32)
    filled = lax.dynamic_update_slice(filled, make_tiles(own_block[None]), (0, 0, 0))

    def advance(offset, carry):
        moving, result = carry
        moving = from_behind(moving, "tm", -1)
        result = lax.dynamic_update_slice(
            result, make_tiles(moving[None]), (0, 0, offset * frame_rows)
        )
        return (moving, result)

    _, filled = lax.fori_loop(1, slot_total, advance, (own_block, filled))
    return filled


VMEM = pl.BlockSpec(memory_space=pltpu.VMEM)


def local_call(body, outs, count_in, scratch=()):
    return pl.pallas_call(
        body,
        out_shape=outs,
        in_specs=[VMEM] * count_in,
        out_specs=[VMEM] * len(outs),
        scratch_shapes=list(scratch),
        compiler_params=pltpu.CompilerParams(vmem_limit_bytes=VMEM_LIMIT),
    )


def lanes_at(start, width):
    return pl.ds(pl.multiple_of(start, LANES), width)


def pack_kernel(loop, groups, per, first, frames, labels, *outs):
    t, p = lax.axis_index("tm"), lax.axis_index("pix")
    rest = per - first
    to_time, to_owner_first, to_owner_rest = outs[:loop], outs[loop : loop + groups], outs[loop + groups :]

    def tile(index):
        live = jnp.where(labels[pl.ds(index, 1), :] >= 0, 1.0, 0.0).astype(jnp.bfloat16)
        return frames[:, lanes_at(index * LANES, LANES)] * live

    for j in range(loop):
        for g in range(groups):
            for s in range(first):
                at = (g * first + s) * LANES
                to_time[j][:, at : at + LANES] = tile((g * loop + (t ^ j)) * per + s)
    for k in range(groups):
        for c in range(loop):
            for s in range(per):
                value = tile(((p ^ k) * loop + c) * per + s)
                if s < first:
                    at = (c * first + s) * LANES
                    to_owner_first[k][:, at : at + LANES] = value
                else:
                    at = (c * rest + s - first) * LANES
                    to_owner_rest[k][:, at : at + LANES] = value


def pick_kernel(axis, count, width, *refs):
    sources, outs = refs[:count], refs[count:]
    me = lax.axis_index(axis)
    for j, out in enumerate(outs):
        for k, source in enumerate(sources):
            out[k] = source[:, lanes_at((me ^ j) * width, width)]


def padded(value):
    wide = value.astype(jnp.float32)
    live = jnp.where(wide[0:1, :] != 0, 1.0, 0.0)
    return jnp.concatenate([wide, jnp.broadcast_to(live, (8, LANES))], axis=0)


def halves(block):
    lane = lax.broadcasted_iota(jnp.int32, block.shape, 1) % LANES
    zero = jnp.zeros_like(block)
    return jnp.concatenate(
        [jnp.where(lane < CYCLE_CAP, block, zero), jnp.where(lane < CYCLE_CAP, zero, block)], axis=0
    )


def normalized(product, rows):
    result = []
    for half in range(2):
        cycle = product[half * (rows + 8) : (half + 1) * (rows + 8)]
        count = cycle[rows : rows + 1, rows : rows + 1]
        row_scale = count / cycle[:rows, rows : rows + 1]
        column_scale = 1.0 / cycle[rows : rows + 1, :]
        result.append(cycle[:rows] * row_scale * column_scale)
    return result


def dot_rows(left, right):
    return lax.dot_general(
        left, right, (((1,), (1,)), ((), ())), preferred_element_type=jnp.float32
    )


def cross_kernel(loop, groups, pairs, rows, time_major, *refs):
    count_in = groups if time_major else loop
    sources, outs, blocks = refs[:count_in], refs[count_in : count_in + loop], refs[-1]
    t = lax.axis_index("tm")
    for s in range(pairs):
        at = slice(s * LANES, (s + 1) * LANES)
        for j in range(loop):
            for k in range(groups):
                value = sources[k][j, :, at] if time_major else sources[j][k, :, at]
                blocks[s, t ^ j, :, k * LANES : (k + 1) * LANES] = padded(value).astype(jnp.bfloat16)
        for i in range(loop):
            r = t ^ i
            left = halves(blocks[s, r].astype(jnp.float32)).astype(jnp.bfloat16)
            right = jnp.concatenate(
                [blocks[s, (r + 1) % loop], blocks[s, (r + 2) % loop]], axis=0
            )
            for half, cycle in enumerate(normalized(dot_rows(left, right), rows)):
                outs[i][2 * s + half] = cycle - 1.0


def own_kernel(loop, groups, pairs, rows, *refs):
    sources, out = refs[:groups], refs[groups]
    for c in range(loop):
        for s in range(pairs):
            at = slice((c * pairs + s) * LANES, (c * pairs + s + 1) * LANES)
            block = jnp.concatenate([padded(source[:, at]) for source in sources], axis=1)
            left = halves(block).astype(jnp.bfloat16)
            block = block.astype(jnp.bfloat16)
            right = jnp.concatenate([block, block], axis=0)
            for half, cycle in enumerate(normalized(dot_rows(left, right), rows)):
                out[c, 2 * s + half] = cycle


def place_kernel(rows, counts, me, *refs):
    del me
    out = refs[-1]
    lane = lax.broadcasted_iota(jnp.int32, (rows, LANES), 1)
    base = 0
    for own, cross in zip(refs[0:-1:2], refs[1:-1:2]):
        for c in range(own.shape[1]):
            value = cross[0, c] + 1.0
            one = pltpu.roll(value, rows, 1)
            two = pltpu.roll(value, 2 * rows - CYCLE_CAP, 1)
            out[base + c, :, :LANES] = jnp.where(
                lane < rows, own[0, c], jnp.where(lane < 2 * rows, one, two)
            )
            out[base + c, :, LANES:] = two[:, : 3 * rows - LANES]
        base += own.shape[1]


def spread(frames, labels, first):
    loop, groups = lax.axis_size("tm"), lax.axis_size("pix")
    rows = frames.shape[0]
    per = frames.shape[1] // (LANES * groups * loop)
    rest = per - first
    bf16, f32 = jnp.bfloat16, jnp.float32

    def shape(*dims, dtype=bf16):
        return jax.ShapeDtypeStruct(dims, dtype)

    packed = local_call(
        functools.partial(pack_kernel, loop, groups, per, first),
        [shape(rows, groups * first * LANES)] * loop
        + [shape(rows, loop * first * LANES)] * groups
        + [shape(rows, loop * rest * LANES)] * groups,
        2,
    )(frames, labels.reshape(-1, LANES))
    to_time, to_owner_first, to_owner_rest = packed[:loop], packed[loop : loop + groups], packed[loop + groups :]

    def exchange(parts, axis):
        moved = {j: swap(parts[j], axis, j) for j in range(len(parts) - 1, 0, -1)}
        return [parts[0]] + [moved[j] for j in range(1, len(parts))]

    def pick(parts, axis, width):
        size = lax.axis_size(axis)
        return local_call(
            functools.partial(pick_kernel, axis, len(parts), width),
            [shape(len(parts), rows, width)] * size,
            len(parts),
        )(*parts)

    def cross(parts, pairs, time_major):
        return local_call(
            functools.partial(cross_kernel, loop, groups, pairs, rows, time_major),
            [shape(2 * pairs, rows, LANES, dtype=f32)] * loop,
            len(parts),
            [pltpu.VMEM((pairs, loop, rows + 8, groups * LANES), bf16)],
        )(*parts)

    def send_back(tiles):
        sent = lax.optimization_barrier([tile.astype(jnp.float16) for tile in tiles[1:]])
        moved = {j: swap(sent[j - 1], "tm", j) for j in range(loop - 1, 0, -1)}
        moved = lax.optimization_barrier(moved)
        return jnp.stack([tiles[0]] + [moved[j].astype(f32) for j in range(1, loop)])

    def own(parts, pairs):
        return local_call(
            functools.partial(own_kernel, loop, groups, pairs, rows),
            [shape(loop, 2 * pairs, rows, LANES, dtype=f32)],
            len(parts),
        )(*parts)[0]

    time_first = exchange(to_time, "tm")
    owned_rest = exchange(to_owner_rest, "pix")
    time_rest = exchange(pick(owned_rest, "tm", rest * LANES), "tm")
    grouped_first = exchange(pick(time_first, "pix", first * LANES), "pix")
    owned_first = exchange(to_owner_first, "pix")
    own_rest = own(owned_rest, rest)
    back_first = send_back(cross(grouped_first, first, True))
    back_rest = send_back(cross(time_rest, rest, False))
    own_first = own(owned_first, first)

    me = lax.axis_index("tm").astype(jnp.int32)[None]
    cycles = 2 * per

    def part(pairs, order):
        return pl.BlockSpec((1, 2 * pairs, rows, LANES), order)

    return pl.pallas_call(
        functools.partial(place_kernel, rows, (first, rest)),
        out_shape=shape(loop * cycles, rows, 3 * rows, dtype=f32),
        grid_spec=pltpu.PrefetchScalarGridSpec(
            num_scalar_prefetch=1,
            grid=(loop,),
            in_specs=[
                part(first, lambda i, t: (t[0] ^ i, 0, 0, 0)),
                part(first, lambda i, t: (i, 0, 0, 0)),
                part(rest, lambda i, t: (t[0] ^ i, 0, 0, 0)),
                part(rest, lambda i, t: (i, 0, 0, 0)),
            ],
            out_specs=pl.BlockSpec((cycles, rows, 3 * rows), lambda i, t: (t[0] ^ i, 0, 0)),
        ),
        compiler_params=pltpu.CompilerParams(vmem_limit_bytes=VMEM_LIMIT),
    )(me, own_first, back_first, own_rest, back_rest)


def on_device(frames, labels):
    loop, groups = lax.axis_size("tm"), lax.axis_size("pix")
    pairs = CYCLES // groups // 2
    powers = groups & (groups - 1) == 0
    fits = frames.shape[1] == CYCLES * CYCLE_CAP and frames.shape[0] == CYCLE_CAP - 8
    if loop == 4 and powers and fits and pairs % loop == 0 and pairs // loop >= 2:
        return spread(frames, labels, pairs // loop // 2)
    return ring(frames, labels)


def solution(mesh):
    placed = (P(("runs", "tm"), "pix"), P("pix"))
    return jax.shard_map(
        on_device,
        mesh=mesh,
        in_specs=placed,
        out_specs=P(("runs", "pix"), "tm", None),
        check_vma=False,
    )
```

```python
import functools

import jax
import jax.numpy as jnp
from jax import lax
from jax.experimental import pallas as pl
from jax.experimental.pallas import tpu as pltpu
from jax.sharding import PartitionSpec as P

CYCLES = 128
CYCLE_CAP = 64
LANES = 128
VMEM_LIMIT = 48 * 2**20
OWN_COST, PLACE_COST = 4 << 20, 4 << 20


def from_behind(shard, axis, by):
    size = lax.axis_size(axis)
    return lax.ppermute(shard, axis, [(i, (i + by) % size) for i in range(size)])


def swap(shard, axis, by):
    size = lax.axis_size(axis)
    return lax.ppermute(shard, axis, [(i, i ^ by) for i in range(size)])


def ring(frames, labels):
    groups = lax.axis_size("pix")
    loop_size = lax.axis_size("tm")
    local_cycles = CYCLES // groups
    slot_total = loop_size // 2 + 1
    frame_rows = frames.shape[0]
    live_row = (labels >= 0).astype(jnp.bfloat16)[None, :]
    masked = frames * live_row
    own_block, live_owned = (
        lax.all_to_all(masked, "pix", split_axis=1, concat_axis=1, tiled=True),
        lax.all_to_all(live_row, "pix", split_axis=1, concat_axis=1, tiled=True),
    )

    def split_cycles(values):
        return values.reshape(values.shape[:-1] + (groups, local_cycles, CYCLE_CAP))

    counts = jnp.sum(split_cycles(live_owned).astype(jnp.float32), axis=(0, 1, 3))
    own_split = split_cycles(own_block)
    own_means = jnp.sum(own_split, axis=(1, 3), dtype=jnp.float32) / counts

    def make_tiles(blocks):
        block_split = split_cycles(blocks)
        block_means = jnp.sum(block_split, axis=(2, 4), dtype=jnp.float32) / counts
        gram_tiles = jnp.einsum(
            "tgqc,nsgqc->qtns", own_split, block_split, preferred_element_type=jnp.float32
        )
        denominator = (
            counts[:, None, None, None]
            * own_means.T[:, :, None, None]
            * jnp.transpose(block_means, (2, 0, 1))[:, None, :, :]
        )
        return (gram_tiles / denominator).reshape(
            local_cycles, frame_rows, blocks.shape[0] * frame_rows
        )

    filled = jnp.zeros((local_cycles, frame_rows, slot_total * frame_rows), jnp.float32)
    filled = lax.dynamic_update_slice(filled, make_tiles(own_block[None]), (0, 0, 0))

    def advance(offset, carry):
        moving, result = carry
        moving = from_behind(moving, "tm", -1)
        result = lax.dynamic_update_slice(
            result, make_tiles(moving[None]), (0, 0, offset * frame_rows)
        )
        return (moving, result)

    _, filled = lax.fori_loop(1, slot_total, advance, (own_block, filled))
    return filled


VMEM = pl.BlockSpec(memory_space=pltpu.VMEM)
HBM = pl.BlockSpec(memory_space=pltpu.HBM)
ANY = pl.BlockSpec(memory_space=pl.ANY)


def local_call(body, outs, count_in, scratch=(), in_specs=None, out_specs=None, after=(), cost=1, **options):
    def ordered(*refs):
        body(*refs[: len(refs) - skipped], *refs[len(refs) - tail :])

    tail = len(outs) + len(scratch)
    skipped = tail + len(after)
    call = pl.pallas_call(
        ordered,
        out_shape=outs,
        in_specs=(in_specs or [VMEM] * count_in) + [ANY] * len(after),
        out_specs=out_specs or [VMEM] * len(outs),
        scratch_shapes=list(scratch),
        compiler_params=pltpu.CompilerParams(vmem_limit_bytes=VMEM_LIMIT),
        cost_estimate=pl.CostEstimate(flops=1, bytes_accessed=cost, transcendentals=0),
        **options,
    )
    return lambda *operands: call(*operands, *after)


def lanes_at(start, width):
    return pl.ds(pl.multiple_of(start, LANES), width)


def pack_kernel(loop, groups, per, first, frames, live, *outs):
    t, p = lax.axis_index("tm"), lax.axis_index("pix")
    to_time, to_owner = outs[: loop - 1], outs[loop - 1 :]

    def tile(index):
        return frames[:, lanes_at(index * LANES, LANES)] * live[pl.ds(index, 1), :].astype(jnp.bfloat16)

    for j in range(1, loop):
        for g in range(groups):
            for s in range(first):
                at = (g * first + s) * LANES
                to_time[j - 1][:, at : at + LANES] = tile((g * loop + (t ^ j)) * per + s)
    for k in range(groups):
        for c in range(loop * per):
            to_owner[k][:, c * LANES : (c + 1) * LANES] = tile((p ^ k) * loop * per + c)


def pick_kernel(axis, partners, step, base, width, count, *refs):
    sources, outs = refs[:count][::-1], refs[count:]
    me = lax.axis_index(axis)
    for j, out in zip(partners, outs):
        for k, source in enumerate(sources):
            out[k] = source[:, lanes_at((me ^ j) * step + base, width)]


def padded(value):
    wide = value.astype(jnp.float32)
    live = jnp.where(wide[0:1, :] != 0, 1.0, 0.0)
    return jnp.concatenate([wide, jnp.broadcast_to(live, (8, LANES))], axis=0)


def halves(block):
    lane = lax.broadcasted_iota(jnp.int32, block.shape, 1) % LANES
    zero = jnp.zeros_like(block)
    return jnp.concatenate(
        [jnp.where(lane < CYCLE_CAP, block, zero), jnp.where(lane < CYCLE_CAP, zero, block)], axis=0
    )


def normalized(product, rows):
    result = []
    for half in range(2):
        cycle = product[half * (rows + 8) : (half + 1) * (rows + 8)]
        count = cycle[rows : rows + 1, rows : rows + 1]
        row_scale = count / cycle[:rows, rows : rows + 1]
        column_scale = 1.0 / cycle[rows : rows + 1, :]
        result.append(cycle[:rows] * row_scale * column_scale)
    return result


def dot_rows(left, right):
    return lax.dot_general(
        left, right, (((1,), (1,)), ((), ())), preferred_element_type=jnp.float32
    )


def cross_kernel(loop, groups, per, base, pairs, rows, by_group, *refs):
    sources, outs, blocks = refs[: groups + len(refs) - 1 - loop - groups], refs[-1 - loop : -1], refs[-1]
    own, others = sources[:groups], sources[groups:][::-1]
    t = lax.axis_index("tm")
    for s in range(pairs):
        at = slice(s * LANES, (s + 1) * LANES)
        for j in range(loop):
            for k in range(groups):
                if j == 0:
                    value = own[k][:, lanes_at((t * per + base + s) * LANES, LANES)]
                elif by_group:
                    value = others[k][j - 1, :, at]
                else:
                    value = others[j - 1][k, :, at]
                blocks[s, t ^ j, :, k * LANES : (k + 1) * LANES] = padded(value).astype(jnp.bfloat16)
        for i in range(loop):
            r = t ^ i
            left = halves(blocks[s, r].astype(jnp.float32)).astype(jnp.bfloat16)
            right = jnp.concatenate(
                [blocks[s, (r + 1) % loop], blocks[s, (r + 2) % loop]], axis=0
            )
            for half, cycle in enumerate(normalized(dot_rows(left, right), rows)):
                outs[i][2 * s + half] = cycle - 1.0


def own_kernel(pairs, rows, *refs):
    sources, out = refs[:-1], refs[-1]
    for c in range(pairs):
        at = slice(c * LANES, (c + 1) * LANES)
        block = jnp.concatenate([padded(source[:, at]) for source in sources], axis=1)
        left = halves(block).astype(jnp.bfloat16)
        block = block.astype(jnp.bfloat16)
        right = jnp.concatenate([block, block], axis=0)
        for half, cycle in enumerate(normalized(dot_rows(left, right), rows)):
            out[2 * c + half] = cycle


def place_kernel(loop, rows, pairs, cycles, base, own, *refs):
    parts, (out, slots, sems) = refs[:loop][::-1], refs[-3:]
    t = lax.axis_index("tm")
    lane = lax.broadcasted_iota(jnp.int32, (rows, LANES), 1)
    copies = []
    for i in range(loop):
        at = (t ^ i) * cycles + base
        for c in range(2 * pairs):
            value = parts[i][c] + 1.0
            one = pltpu.roll(value, rows, 1)
            two = pltpu.roll(value, 2 * rows - CYCLE_CAP, 1)
            slots[i, c, :, :LANES] = jnp.where(
                lane < rows, own[at + c], jnp.where(lane < 2 * rows, one, two)
            )
            slots[i, c, :, LANES:] = two[:, : 3 * rows - LANES]
        copies.append(
            pltpu.make_async_copy(slots.at[i], out.at[pl.ds(at, 2 * pairs)], sems.at[i])
        )
        copies[-1].start()
    for copy in copies:
        copy.wait()


def spread(frames, labels, first):
    loop, groups = lax.axis_size("tm"), lax.axis_size("pix")
    rows = frames.shape[0]
    per = frames.shape[1] // (LANES * groups * loop)
    rest = per - first
    cycles = 2 * per
    bf16, f32 = jnp.bfloat16, jnp.float32

    def shape(*dims, dtype=bf16):
        return jax.ShapeDtypeStruct(dims, dtype)

    packed = local_call(
        functools.partial(pack_kernel, loop, groups, per, first),
        [shape(rows, groups * first * LANES)] * (loop - 1) + [shape(rows, loop * per * LANES)] * groups,
        2,
    )(frames, jnp.where(labels >= 0, 1.0, 0.0).astype(f32).reshape(-1, LANES))

    def exchange(parts, axis):
        return [swap(part, axis, j) for j, part in enumerate(parts, 1)]

    def over_pix(parts):
        over = swap(parts[2], "pix", 2)
        next_core = swap(parts[3], "pix", 1)
        core = swap(parts[1], "pix", 1)
        return [parts[0], core, over, swap(next_core, "pix", 2)]

    def pick(parts, axis, partners, step, base, width):
        return local_call(
            functools.partial(pick_kernel, axis, partners, step, base, width, len(parts)),
            [shape(len(parts), rows, width)] * len(partners),
            len(parts),
        )(*parts[::-1])

    def cross(own, others, base, pairs, by_group, after=()):
        return local_call(
            functools.partial(cross_kernel, loop, groups, per, base, pairs, rows, by_group),
            [shape(2 * pairs, rows, LANES, dtype=f32)] * loop,
            groups + len(others),
            [pltpu.VMEM((pairs, loop, rows + 8, groups * LANES), bf16)],
            after=after,
        )(*own, *others[::-1])

    def block(body, *operands):
        here = lax.axis_index("tm") < loop
        outs = jax.eval_shape(body, *operands)
        return lax.cond(
            here, body, lambda *_: jax.tree.map(lambda o: jnp.zeros(o.shape, o.dtype), outs), *operands
        )

    def first_to_owner(own, arrived, after):
        del after
        picked = pick(arrived, "pix", range(groups), first * LANES, 0, first * LANES)
        return cross(own, over_pix(picked), 0, first, True)

    def send_back(tiles):
        sent = lax.optimization_barrier([tile.astype(jnp.float16) for tile in tiles[1:]])
        moved = lax.optimization_barrier(exchange(sent, "tm"))
        return [tiles[0]] + [tile.astype(f32) for tile in moved]

    def place(base, pairs, tiles, filled, cost):
        return local_call(
            functools.partial(place_kernel, loop, rows, pairs, cycles, base),
            [shape(loop * cycles, rows, 3 * rows, dtype=f32)],
            1 + len(tiles) + len(filled),
            [pltpu.VMEM((loop, 2 * pairs, rows, 3 * rows), f32), pltpu.SemaphoreType.DMA((loop,))],
            in_specs=[VMEM] * (1 + len(tiles)) + [HBM] * len(filled),
            out_specs=[HBM],
            input_output_aliases={1 + len(tiles): 0} if filled else {},
            cost=cost,
        )(own_tiles, *tiles[::-1], *filled)[0]

    time_first = exchange(packed[: loop - 1], "tm")
    mine, *to_owner = packed[loop - 1 :]
    owned = [mine] + exchange(to_owner, "pix")
    picked_rest = pick(owned, "tm", range(1, loop), per * LANES, first * LANES, rest * LANES)
    time_rest = exchange(picked_rest, "tm")
    tiles_first = block(first_to_owner, owned, time_first, picked_rest[:1])
    tiles_rest = cross(owned, time_rest, first, rest, False, tiles_first[:1])
    own_tiles = local_call(
        functools.partial(own_kernel, loop * per, rows),
        [shape(loop * cycles, rows, LANES, dtype=f32)],
        groups,
        cost=OWN_COST,
    )(*owned)[0]
    back_first = send_back(tiles_first)
    back_rest = send_back(tiles_rest)
    filled = place(0, first, back_first, (), PLACE_COST)
    return place(2 * first, rest, back_rest, (filled,), PLACE_COST)


def on_device(frames, labels):
    loop, groups = lax.axis_size("tm"), lax.axis_size("pix")
    pairs = CYCLES // groups // 2
    fits = frames.shape[1] == CYCLES * CYCLE_CAP and frames.shape[0] == CYCLE_CAP - 8
    if loop == 4 and groups == 4 and fits and pairs % loop == 0 and pairs // loop >= 2:
        return spread(frames, labels, pairs // loop // 2)
    return ring(frames, labels)


def solution(mesh):
    placed = (P(("runs", "tm"), "pix"), P("pix"))
    return jax.shard_map(
        on_device,
        mesh=mesh,
        in_specs=placed,
        out_specs=P(("runs", "pix"), "tm", None),
        check_vma=False,
    )
```

```python
import functools

import jax
import jax.numpy as jnp
from jax import lax
from jax.experimental import pallas as pl
from jax.experimental.pallas import tpu as pltpu
from jax.sharding import PartitionSpec as P

CYCLES = 128
CYCLE_CAP = 64
LANES = 128
PIECE = 16
VMEM_LIMIT = 48 * 2**20
OWN_COST, PLACE_COST = 4 << 20, 4 << 20


def from_behind(shard, axis, by):
    size = lax.axis_size(axis)
    return lax.ppermute(shard, axis, [(i, (i + by) % size) for i in range(size)])


def swap(shard, axis, by):
    size = lax.axis_size(axis)
    return lax.ppermute(shard, axis, [(i, i ^ by) for i in range(size)])


def ring(frames, labels):
    groups = lax.axis_size("pix")
    loop_size = lax.axis_size("tm")
    local_cycles = CYCLES // groups
    slot_total = loop_size // 2 + 1
    frame_rows = frames.shape[0]
    live_row = (labels >= 0).astype(jnp.bfloat16)[None, :]
    masked = frames * live_row
    own_block, live_owned = (
        lax.all_to_all(masked, "pix", split_axis=1, concat_axis=1, tiled=True),
        lax.all_to_all(live_row, "pix", split_axis=1, concat_axis=1, tiled=True),
    )

    def split_cycles(values):
        return values.reshape(values.shape[:-1] + (groups, local_cycles, CYCLE_CAP))

    counts = jnp.sum(split_cycles(live_owned).astype(jnp.float32), axis=(0, 1, 3))
    own_split = split_cycles(own_block)
    own_means = jnp.sum(own_split, axis=(1, 3), dtype=jnp.float32) / counts

    def make_tiles(blocks):
        block_split = split_cycles(blocks)
        block_means = jnp.sum(block_split, axis=(2, 4), dtype=jnp.float32) / counts
        gram_tiles = jnp.einsum(
            "tgqc,nsgqc->qtns", own_split, block_split, preferred_element_type=jnp.float32
        )
        denominator = (
            counts[:, None, None, None]
            * own_means.T[:, :, None, None]
            * jnp.transpose(block_means, (2, 0, 1))[:, None, :, :]
        )
        return (gram_tiles / denominator).reshape(
            local_cycles, frame_rows, blocks.shape[0] * frame_rows
        )

    filled = jnp.zeros((local_cycles, frame_rows, slot_total * frame_rows), jnp.float32)
    filled = lax.dynamic_update_slice(filled, make_tiles(own_block[None]), (0, 0, 0))

    def advance(offset, carry):
        moving, result = carry
        moving = from_behind(moving, "tm", -1)
        result = lax.dynamic_update_slice(
            result, make_tiles(moving[None]), (0, 0, offset * frame_rows)
        )
        return (moving, result)

    _, filled = lax.fori_loop(1, slot_total, advance, (own_block, filled))
    return filled


VMEM = pl.BlockSpec(memory_space=pltpu.VMEM)
HBM = pl.BlockSpec(memory_space=pltpu.HBM)
ANY = pl.BlockSpec(memory_space=pl.ANY)


def local_call(body, outs, count_in, scratch=(), in_specs=None, out_specs=None, after=(), cost=1, **options):
    def ordered(*refs):
        body(*refs[: len(refs) - skipped], *refs[len(refs) - tail :])

    tail = len(outs) + len(scratch)
    skipped = tail + len(after)
    call = pl.pallas_call(
        ordered,
        out_shape=outs,
        in_specs=(in_specs or [VMEM] * count_in) + [ANY] * len(after),
        out_specs=out_specs or [VMEM] * len(outs),
        scratch_shapes=list(scratch),
        compiler_params=pltpu.CompilerParams(vmem_limit_bytes=VMEM_LIMIT),
        cost_estimate=pl.CostEstimate(flops=1, bytes_accessed=cost, transcendentals=0),
        **options,
    )
    return lambda *operands: call(*operands, *after)


def lanes_at(start, width):
    return pl.ds(pl.multiple_of(start, LANES), width)


def pack_kernel(loop, groups, per, frames, live, mine, over, core):
    p = lax.axis_index("pix")
    for k, out in ((1, core.at[0]), (3, core.at[1]), (0, mine), (2, over)):
        for n in range(loop * per):
            index = (p ^ k) * loop * per + n
            mask = live[pl.ds(index, 1), :].astype(jnp.bfloat16)
            out[:, n * LANES : (n + 1) * LANES] = frames[:, lanes_at(index * LANES, LANES)] * mask


def near_kernel(loop, per, parts, mine, over, core, *outs):
    t = lax.axis_index("tm")
    to_chip, to_time = outs[: len(parts)], outs[len(parts) :]
    for j, out in enumerate(to_time, 1):
        lanes = lanes_at((t ^ j) * per * LANES, per * LANES)
        out[0] = mine[:, lanes]
        out[1] = core[0, :, lanes]
    for (start, count), out in zip(parts, to_chip):
        for c in range(loop):
            source = slice((c * per + start) * LANES, (c * per + start + count) * LANES)
            target = slice(c * count * LANES, (c + 1) * count * LANES)
            out[0, :, target] = over[:, source]
            out[1, :, target] = core[1, :, source]


def far_kernel(count, chip, *outs):
    t = lax.axis_index("tm")
    for j, out in enumerate(outs, 1):
        out[...] = chip[:, :, lanes_at((t ^ j) * count * LANES, count * LANES)]


def padded(value):
    wide = value.astype(jnp.float32)
    live = jnp.where(wide[0:1, :] != 0, 1.0, 0.0)
    return jnp.concatenate([wide, jnp.broadcast_to(live, (8, LANES))], axis=0)


def halves(block):
    lane = lax.broadcasted_iota(jnp.int32, block.shape, 1) % LANES
    zero = jnp.zeros_like(block)
    return jnp.concatenate(
        [jnp.where(lane < CYCLE_CAP, block, zero), jnp.where(lane < CYCLE_CAP, zero, block)], axis=0
    )


def normalized(product, rows):
    result = []
    for half in range(2):
        cycle = product[half * (rows + 8) : (half + 1) * (rows + 8)]
        count = cycle[rows : rows + 1, rows : rows + 1]
        row_scale = count / cycle[:rows, rows : rows + 1]
        column_scale = 1.0 / cycle[rows : rows + 1, :]
        result.append(cycle[:rows] * row_scale * column_scale)
    return result


def dot_rows(left, right):
    return lax.dot_general(
        left, right, (((1,), (1,)), ((), ())), preferred_element_type=jnp.float32
    )


def lane_of(rows):
    return lax.broadcasted_iota(jnp.int32, (rows, LANES), 1)


def cross_kernel(loop, per, part, rows, last, mine, core, chip, *refs):
    start, count = part
    near, far = refs[: loop - 1][::-1], refs[loop - 1 : 2 * loop - 2][::-1]
    early, outs, blocks = refs[2 * loop - 2 : -1 - loop], refs[-1 - loop : -1], refs[-1]
    t = lax.axis_index("tm")
    lane = lane_of(rows)
    before = 2 * start if last else 0

    def put(i, cycle, tile):
        if not last or i == 0 or cycle < 2 * per - 1:
            outs[i][cycle] = tile
        else:
            for m in range(cycle):
                spare = pltpu.roll(tile, (2 * rows - PIECE * m) % LANES, 1)
                outs[i][m] = jnp.where(lane < 2 * rows, outs[i][m], spare)

    for n, tiles in enumerate(early):
        for c in range(tiles.shape[0]):
            put(n % loop, n // loop * tiles.shape[0] + c, tiles[c])
    for s in range(count):
        at = lanes_at((t * per + start + s) * LANES, LANES)
        at_near = slice((start + s) * LANES, (start + s + 1) * LANES)
        at_far = slice(s * LANES, (s + 1) * LANES)
        at_chip = lanes_at((t * count + s) * LANES, LANES)
        for j in range(loop):
            if j == 0:
                values = mine[:, at], core[0, :, at], chip[0, :, at_chip], chip[1, :, at_chip]
            else:
                values = [near[j - 1][k, :, at_near] for k in range(2)] + [far[j - 1][k, :, at_far] for k in range(2)]
            for k, value in enumerate(values):
                blocks[s, t ^ j, :, k * LANES : (k + 1) * LANES] = padded(value).astype(jnp.bfloat16)
        for i in range(loop):
            r = t ^ i
            left = halves(blocks[s, r].astype(jnp.float32)).astype(jnp.bfloat16)
            right = jnp.concatenate(
                [blocks[s, (r + 1) % loop], blocks[s, (r + 2) % loop]], axis=0
            )
            for half, cycle in enumerate(normalized(dot_rows(left, right), rows)):
                cycle = cycle - 1.0
                cycle = jnp.where(lane < rows, cycle, pltpu.roll(cycle, LANES + rows - CYCLE_CAP, 1))
                put(i, before + 2 * s + half, cycle)


def own_kernel(loop, per, parts, rows, mine, core, *refs):
    chips, out = refs[:-1], refs[-1]
    for c in range(loop):
        for (start, count), chip in zip(parts, chips):
            for s in range(count):
                n = c * per + start + s
                at = slice(n * LANES, (n + 1) * LANES)
                at_chip = slice((c * count + s) * LANES, (c * count + s + 1) * LANES)
                values = mine[:, at], core[0, :, at], chip[0, :, at_chip], chip[1, :, at_chip]
                block = jnp.concatenate([padded(value) for value in values], axis=1)
                left = halves(block).astype(jnp.bfloat16)
                block = block.astype(jnp.bfloat16)
                right = jnp.concatenate([block, block], axis=0)
                for half, cycle in enumerate(normalized(dot_rows(left, right), rows)):
                    out[2 * n + half] = cycle


def place_kernel(rows, cycles, partners, own, *refs):
    tiles, (out, slots, sems) = refs[: len(partners)], refs[-3:]
    t = lax.axis_index("tm")
    lane = lane_of(rows)
    copies = []
    for n, (i, part) in enumerate(zip(partners, tiles)):
        at = (t ^ i) * cycles
        for c in range(cycles):
            if c < part.shape[0]:
                value = part[c]
            else:
                value = jnp.zeros((rows, LANES), jnp.float32)
                for m in range(c):
                    piece = pltpu.roll(part[m], PIECE * (m + 1) % LANES, 1)
                    value = jnp.where(lane // PIECE == m, piece, value)
            value = pltpu.roll(value + 1.0, rows, 1)
            slots[n, c, :, :LANES] = jnp.where(lane < rows, own[at + c], value)
            slots[n, c, :, LANES:] = value[:, : 3 * rows - LANES]
        copies.append(pltpu.make_async_copy(slots.at[n], out.at[pl.ds(at, cycles)], sems.at[n]))
        copies[-1].start()
    for copy in copies:
        copy.wait()


def spread(frames, labels, counts):
    loop, groups = lax.axis_size("tm"), lax.axis_size("pix")
    rows = frames.shape[0]
    per = frames.shape[1] // (LANES * groups * loop)
    cycles = 2 * per
    bf16, f32 = jnp.bfloat16, jnp.float32
    parts = [(sum(counts[:n]), count) for n, count in enumerate(counts)]

    def shape(*dims, dtype=bf16):
        return jax.ShapeDtypeStruct(dims, dtype)

    def tiles(count):
        return shape(count, rows, LANES, dtype=f32)

    mine, over, core = local_call(
        functools.partial(pack_kernel, loop, groups, per),
        [shape(rows, loop * per * LANES)] * 2 + [shape(2, rows, loop * per * LANES)],
        2,
    )(frames, jnp.where(labels >= 0, 1.0, 0.0).astype(f32).reshape(-1, LANES))
    core = swap(core, "pix", 1)
    ready = local_call(
        functools.partial(near_kernel, loop, per, parts),
        [shape(2, rows, loop * count * LANES) for _, count in parts]
        + [shape(2, rows, per * LANES)] * (loop - 1),
        3,
    )(mine, over, core)
    chips = [swap(part, "pix", 2) for part in ready[: len(parts)]]
    near = [swap(part, "tm", j) for j, part in enumerate(ready[len(parts) :], 1)]
    early = []
    for part, chip in zip(parts, chips):
        far = local_call(
            functools.partial(far_kernel, part[1]), [shape(2, rows, part[1] * LANES)] * (loop - 1), 1
        )(chip)
        far = [swap(value, "tm", j) for j, value in enumerate(far, 1)]
        last = part is parts[-1]
        early += local_call(
            functools.partial(cross_kernel, loop, per, part, rows, last),
            [tiles(cycles)] + [tiles(cycles - 1)] * (loop - 1) if last else [tiles(2 * part[1])] * loop,
            2 * loop + 1 + (len(early) if last else 0),
            [pltpu.VMEM((part[1], loop, rows + 8, groups * LANES), bf16)],
        )(mine, core, chip, *near[::-1], *far[::-1], *(early if last else ()))
    kept, *sent = early[-loop:]
    own_tiles = local_call(
        functools.partial(own_kernel, loop, per, parts, rows),
        [tiles(loop * cycles)],
        2 + len(parts),
        cost=OWN_COST,
    )(mine, core, *chips)[0]
    sent = lax.optimization_barrier([part.astype(jnp.float16) for part in sent])
    back = [lax.optimization_barrier(swap(part, "tm", j)) for j, part in enumerate(sent, 1)]
    one, two, three = [part.astype(f32) for part in back]

    def place(partners, parts, *filled):
        return local_call(
            functools.partial(place_kernel, rows, cycles, partners),
            [shape(loop * cycles, rows, 3 * rows, dtype=f32)],
            1 + len(parts) + len(filled),
            [
                pltpu.VMEM((len(partners), cycles, rows, 3 * rows), f32),
                pltpu.SemaphoreType.DMA((len(partners),)),
            ],
            in_specs=[VMEM] * (1 + len(parts)) + [HBM] * len(filled),
            out_specs=[HBM],
            input_output_aliases={1 + len(parts): 0} if filled else {},
            cost=PLACE_COST,
        )(own_tiles, *parts, *filled)[0]

    return place((2,), (two,), place((0, 1, 3), (kept, one, three)))


def on_device(frames, labels):
    loop, groups = lax.axis_size("tm"), lax.axis_size("pix")
    pairs = CYCLES // groups // 2
    fits = frames.shape[1] == CYCLES * CYCLE_CAP and frames.shape[0] == CYCLE_CAP - 8
    if loop == 4 and groups == 4 and fits and pairs // loop == 4 and pairs % loop == 0:
        return spread(frames, labels, (2, 2))
    return ring(frames, labels)


def solution(mesh):
    placed = (P(("runs", "tm"), "pix"), P("pix"))
    return jax.shard_map(
        on_device,
        mesh=mesh,
        in_specs=placed,
        out_specs=P(("runs", "pix"), "tm", None),
        check_vma=False,
    )
```

```python
import functools

import jax
import jax.numpy as jnp
from jax import lax
from jax.experimental import pallas as pl
from jax.experimental.pallas import tpu as pltpu
from jax.sharding import PartitionSpec as P

CYCLES = 128
CYCLE_CAP = 64
LANES = 128
PIECE = 16
VMEM_LIMIT = 48 * 2**20
OWN_COST, PLACE_COST = 4 << 20, 4 << 20


def from_behind(shard, axis, by):
    size = lax.axis_size(axis)
    return lax.ppermute(shard, axis, [(i, (i + by) % size) for i in range(size)])


def swap(shard, axis, by):
    size = lax.axis_size(axis)
    return lax.ppermute(shard, axis, [(i, i ^ by) for i in range(size)])


def ring(frames, labels):
    groups = lax.axis_size("pix")
    loop_size = lax.axis_size("tm")
    local_cycles = CYCLES // groups
    slot_total = loop_size // 2 + 1
    frame_rows = frames.shape[0]
    live_row = (labels >= 0).astype(jnp.bfloat16)[None, :]
    masked = frames * live_row
    own_block, live_owned = (
        lax.all_to_all(masked, "pix", split_axis=1, concat_axis=1, tiled=True),
        lax.all_to_all(live_row, "pix", split_axis=1, concat_axis=1, tiled=True),
    )

    def split_cycles(values):
        return values.reshape(values.shape[:-1] + (groups, local_cycles, CYCLE_CAP))

    counts = jnp.sum(split_cycles(live_owned).astype(jnp.float32), axis=(0, 1, 3))
    own_split = split_cycles(own_block)
    own_means = jnp.sum(own_split, axis=(1, 3), dtype=jnp.float32) / counts

    def make_tiles(blocks):
        block_split = split_cycles(blocks)
        block_means = jnp.sum(block_split, axis=(2, 4), dtype=jnp.float32) / counts
        gram_tiles = jnp.einsum(
            "tgqc,nsgqc->qtns", own_split, block_split, preferred_element_type=jnp.float32
        )
        denominator = (
            counts[:, None, None, None]
            * own_means.T[:, :, None, None]
            * jnp.transpose(block_means, (2, 0, 1))[:, None, :, :]
        )
        return (gram_tiles / denominator).reshape(
            local_cycles, frame_rows, blocks.shape[0] * frame_rows
        )

    filled = jnp.zeros((local_cycles, frame_rows, slot_total * frame_rows), jnp.float32)
    filled = lax.dynamic_update_slice(filled, make_tiles(own_block[None]), (0, 0, 0))

    def advance(offset, carry):
        moving, result = carry
        moving = from_behind(moving, "tm", -1)
        result = lax.dynamic_update_slice(
            result, make_tiles(moving[None]), (0, 0, offset * frame_rows)
        )
        return (moving, result)

    _, filled = lax.fori_loop(1, slot_total, advance, (own_block, filled))
    return filled


VMEM = pl.BlockSpec(memory_space=pltpu.VMEM)
HBM = pl.BlockSpec(memory_space=pltpu.HBM)
ANY = pl.BlockSpec(memory_space=pl.ANY)


def local_call(body, outs, count_in, scratch=(), in_specs=None, out_specs=None, after=(), cost=1, **options):
    def ordered(*refs):
        body(*refs[: len(refs) - skipped], *refs[len(refs) - tail :])

    tail = len(outs) + len(scratch)
    skipped = tail + len(after)
    call = pl.pallas_call(
        ordered,
        out_shape=outs,
        in_specs=(in_specs or [VMEM] * count_in) + [ANY] * len(after),
        out_specs=out_specs or [VMEM] * len(outs),
        scratch_shapes=list(scratch),
        compiler_params=pltpu.CompilerParams(vmem_limit_bytes=VMEM_LIMIT),
        cost_estimate=pl.CostEstimate(flops=1, bytes_accessed=cost, transcendentals=0),
        **options,
    )
    return lambda *operands: call(*operands, *after)


def lanes_at(start, width):
    return pl.ds(pl.multiple_of(start, LANES), width)


def pack_kernel(loop, groups, per, frames, live, mine, over, core):
    p = lax.axis_index("pix")
    for k, out in ((1, core.at[0]), (3, core.at[1]), (0, mine), (2, over)):
        for n in range(loop * per):
            index = (p ^ k) * loop * per + n
            mask = live[pl.ds(index, 1), :].astype(jnp.bfloat16)
            out[:, n * LANES : (n + 1) * LANES] = frames[:, lanes_at(index * LANES, LANES)] * mask


def near_kernel(loop, per, parts, mine, over, core, *outs):
    t = lax.axis_index("tm")
    to_chip, to_time = outs[: len(parts)], outs[len(parts) :]
    for j, out in enumerate(to_time, 1):
        lanes = lanes_at((t ^ j) * per * LANES, per * LANES)
        out[0] = mine[:, lanes]
        out[1] = core[0, :, lanes]
    for (start, count), out in zip(parts, to_chip):
        for c in range(loop):
            source = slice((c * per + start) * LANES, (c * per + start + count) * LANES)
            target = slice(c * count * LANES, (c + 1) * count * LANES)
            out[0, :, target] = over[:, source]
            out[1, :, target] = core[1, :, source]


def far_kernel(count, chip, *outs):
    t = lax.axis_index("tm")
    for j, out in enumerate(outs, 1):
        out[...] = chip[:, :, lanes_at((t ^ j) * count * LANES, count * LANES)]


def padded(value):
    wide = value.astype(jnp.float32)
    live = jnp.where(wide[0:1, :] != 0, 1.0, 0.0)
    return jnp.concatenate([wide, jnp.broadcast_to(live, (8, LANES))], axis=0)


def halves(block):
    lane = lax.broadcasted_iota(jnp.int32, block.shape, 1) % LANES
    zero = jnp.zeros_like(block)
    return jnp.concatenate(
        [jnp.where(lane < CYCLE_CAP, block, zero), jnp.where(lane < CYCLE_CAP, zero, block)], axis=0
    )


def normalized(product, rows):
    result = []
    for half in range(2):
        cycle = product[half * (rows + 8) : (half + 1) * (rows + 8)]
        count = cycle[rows : rows + 1, rows : rows + 1]
        row_scale = count / cycle[:rows, rows : rows + 1]
        column_scale = 1.0 / cycle[rows : rows + 1, :]
        result.append(cycle[:rows] * row_scale * column_scale)
    return result


def dot_rows(left, right):
    return lax.dot_general(
        left, right, (((1,), (1,)), ((), ())), preferred_element_type=jnp.float32
    )


def lane_of(rows):
    return lax.broadcasted_iota(jnp.int32, (rows, LANES), 1)


def cross_kernel(loop, per, part, rows, last, mine, core, chip, *refs):
    start, count = part
    near, far = refs[: loop - 1][::-1], refs[loop - 1 : 2 * loop - 2][::-1]
    early, outs, blocks = refs[2 * loop - 2 : -1 - loop], refs[-1 - loop : -1], refs[-1]
    t = lax.axis_index("tm")
    lane = lane_of(rows)
    for s in range(count):
        at = lanes_at((t * per + start + s) * LANES, LANES)
        at_near = slice((start + s) * LANES, (start + s + 1) * LANES)
        at_far = slice(s * LANES, (s + 1) * LANES)
        at_chip = lanes_at((t * count + s) * LANES, LANES)
        for j in range(loop):
            if j == 0:
                values = mine[:, at], core[0, :, at], chip[0, :, at_chip], chip[1, :, at_chip]
            else:
                values = [near[j - 1][k, :, at_near] for k in range(2)] + [far[j - 1][k, :, at_far] for k in range(2)]
            for k, value in enumerate(values):
                blocks[s, t ^ j, :, k * LANES : (k + 1) * LANES] = padded(value).astype(jnp.bfloat16)
    products = {}
    for i in range(loop):
        r = t ^ i
        for s in range(count):
            left = halves(blocks[s, r].astype(jnp.float32)).astype(jnp.bfloat16)
            right = jnp.concatenate(
                [blocks[s, (r + 1) % loop], blocks[s, (r + 2) % loop]], axis=0
            )
            products[i, s] = dot_rows(left, right)
    for i, out in enumerate(outs):
        new = []
        for s in range(count):
            for tile in normalized(products[i, s], rows):
                tile = tile - 1.0
                new.append(jnp.where(lane < rows, tile, pltpu.roll(tile, LANES + rows - CYCLE_CAP, 1)))
        before = [tiles[c] for tiles in early[i::loop] for c in range(tiles.shape[0])]
        if last and i:
            spare = new.pop()
            for m, tile in enumerate(before + new):
                out[m] = jnp.where(lane < 2 * rows, tile, pltpu.roll(spare, (2 * rows - PIECE * m) % LANES, 1))
        else:
            for c, tile in enumerate(before + new):
                out[c] = tile


def own_kernel(loop, per, parts, rows, mine, core, *refs):
    chips, out = refs[:-1], refs[-1]
    for c in range(loop):
        for (start, count), chip in zip(parts, chips):
            for s in range(count):
                n = c * per + start + s
                at = slice(n * LANES, (n + 1) * LANES)
                at_chip = slice((c * count + s) * LANES, (c * count + s + 1) * LANES)
                values = mine[:, at], core[0, :, at], chip[0, :, at_chip], chip[1, :, at_chip]
                block = jnp.concatenate([padded(value) for value in values], axis=1)
                left = halves(block).astype(jnp.bfloat16)
                block = block.astype(jnp.bfloat16)
                right = jnp.concatenate([block, block], axis=0)
                for half, cycle in enumerate(normalized(dot_rows(left, right), rows)):
                    out[2 * n + half] = cycle


def place_kernel(rows, cycles, partners, own, *refs):
    tiles, (out, slots, sems) = refs[: len(partners)], refs[-3:]
    t = lax.axis_index("tm")
    lane = lane_of(rows)
    copies = []
    for n, (i, part) in enumerate(zip(partners, tiles)):
        at = (t ^ i) * cycles
        for c in range(cycles):
            if c < part.shape[0]:
                value = part[c]
            else:
                value = jnp.zeros((rows, LANES), jnp.float32)
                for m in range(c):
                    piece = pltpu.roll(part[m], PIECE * (m + 1) % LANES, 1)
                    value = jnp.where(lane // PIECE == m, piece, value)
            value = pltpu.roll(value + 1.0, rows, 1)
            slots[n, c, :, :LANES] = jnp.where(lane < rows, own[at + c], value)
            slots[n, c, :, LANES:] = value[:, : 3 * rows - LANES]
        copies.append(pltpu.make_async_copy(slots.at[n], out.at[pl.ds(at, cycles)], sems.at[n]))
        copies[-1].start()
    for copy in copies:
        copy.wait()


def spread(frames, labels, counts):
    loop, groups = lax.axis_size("tm"), lax.axis_size("pix")
    rows = frames.shape[0]
    per = frames.shape[1] // (LANES * groups * loop)
    cycles = 2 * per
    bf16, f32 = jnp.bfloat16, jnp.float32
    parts = [(sum(counts[:n]), count) for n, count in enumerate(counts)]

    def shape(*dims, dtype=bf16):
        return jax.ShapeDtypeStruct(dims, dtype)

    def tiles(count):
        return shape(count, rows, LANES, dtype=f32)

    mine, over, core = local_call(
        functools.partial(pack_kernel, loop, groups, per),
        [shape(rows, loop * per * LANES)] * 2 + [shape(2, rows, loop * per * LANES)],
        2,
    )(frames, jnp.where(labels >= 0, 1.0, 0.0).astype(f32).reshape(-1, LANES))
    core = swap(core, "pix", 1)
    ready = local_call(
        functools.partial(near_kernel, loop, per, parts),
        [shape(2, rows, loop * count * LANES) for _, count in parts]
        + [shape(2, rows, per * LANES)] * (loop - 1),
        3,
    )(mine, over, core)
    chips = [swap(part, "pix", 2) for part in ready[: len(parts)]]
    near = [swap(part, "tm", j) for j, part in enumerate(ready[len(parts) :], 1)]
    early = []
    for part, chip in zip(parts, chips):
        far = local_call(
            functools.partial(far_kernel, part[1]), [shape(2, rows, part[1] * LANES)] * (loop - 1), 1
        )(chip)
        far = [swap(value, "tm", j) for j, value in enumerate(far, 1)]
        last = part is parts[-1]
        early += local_call(
            functools.partial(cross_kernel, loop, per, part, rows, last),
            [tiles(cycles)] + [tiles(cycles - 1)] * (loop - 1) if last else [tiles(2 * part[1])] * loop,
            2 * loop + 1 + (len(early) if last else 0),
            [pltpu.VMEM((part[1], loop, rows + 8, groups * LANES), bf16)],
        )(mine, core, chip, *near[::-1], *far[::-1], *(early if last else ()))
    kept, *sent = early[-loop:]
    own_tiles = local_call(
        functools.partial(own_kernel, loop, per, parts, rows),
        [tiles(loop * cycles)],
        2 + len(parts),
        cost=OWN_COST,
    )(mine, core, *chips)[0]
    sent = lax.optimization_barrier([part.astype(jnp.float16) for part in sent])
    back = [lax.optimization_barrier(swap(part, "tm", j)) for j, part in enumerate(sent, 1)]
    one, two, three = [part.astype(f32) for part in back]

    def place(partners, parts, *filled):
        return local_call(
            functools.partial(place_kernel, rows, cycles, partners),
            [shape(loop * cycles, rows, 3 * rows, dtype=f32)],
            1 + len(parts) + len(filled),
            [
                pltpu.VMEM((len(partners), cycles, rows, 3 * rows), f32),
                pltpu.SemaphoreType.DMA((len(partners),)),
            ],
            in_specs=[VMEM] * (1 + len(parts)) + [HBM] * len(filled),
            out_specs=[HBM],
            input_output_aliases={1 + len(parts): 0} if filled else {},
            cost=PLACE_COST,
        )(own_tiles, *parts, *filled)[0]

    return place((2, 1), (two, one), place((0, 3), (kept, three)))


def on_device(frames, labels):
    loop, groups = lax.axis_size("tm"), lax.axis_size("pix")
    pairs = CYCLES // groups // 2
    fits = frames.shape[1] == CYCLES * CYCLE_CAP and frames.shape[0] == CYCLE_CAP - 8
    if loop == 4 and groups == 4 and fits and pairs // loop == 4 and pairs % loop == 0:
        return spread(frames, labels, (2, 2))
    return ring(frames, labels)


def solution(mesh):
    placed = (P(("runs", "tm"), "pix"), P("pix"))
    return jax.shard_map(
        on_device,
        mesh=mesh,
        in_specs=placed,
        out_specs=P(("runs", "pix"), "tm", None),
        check_vma=False,
    )
```

```python
import functools

import jax
import jax.numpy as jnp
from jax import lax
from jax.experimental import pallas as pl
from jax.experimental.pallas import tpu as pltpu
from jax.sharding import PartitionSpec as P

CYCLES = 128
CYCLE_CAP = 64
LANES = 128
PIECE = 16
NEAR, FAR = (3, 2, 1), (2, 3, 1)
VMEM_LIMIT = 48 * 2**20
OWN_COST, PLACE_COST = 4 << 20, 4 << 20


def from_behind(shard, axis, by):
    size = lax.axis_size(axis)
    return lax.ppermute(shard, axis, [(i, (i + by) % size) for i in range(size)])


def swap(shard, axis, by):
    size = lax.axis_size(axis)
    return lax.ppermute(shard, axis, [(i, i ^ by) for i in range(size)])


def ring(frames, labels):
    groups = lax.axis_size("pix")
    loop_size = lax.axis_size("tm")
    local_cycles = CYCLES // groups
    slot_total = loop_size // 2 + 1
    frame_rows = frames.shape[0]
    live_row = (labels >= 0).astype(jnp.bfloat16)[None, :]
    masked = frames * live_row
    own_block, live_owned = (
        lax.all_to_all(masked, "pix", split_axis=1, concat_axis=1, tiled=True),
        lax.all_to_all(live_row, "pix", split_axis=1, concat_axis=1, tiled=True),
    )

    def split_cycles(values):
        return values.reshape(values.shape[:-1] + (groups, local_cycles, CYCLE_CAP))

    counts = jnp.sum(split_cycles(live_owned).astype(jnp.float32), axis=(0, 1, 3))
    own_split = split_cycles(own_block)
    own_means = jnp.sum(own_split, axis=(1, 3), dtype=jnp.float32) / counts

    def make_tiles(blocks):
        block_split = split_cycles(blocks)
        block_means = jnp.sum(block_split, axis=(2, 4), dtype=jnp.float32) / counts
        gram_tiles = jnp.einsum(
            "tgqc,nsgqc->qtns", own_split, block_split, preferred_element_type=jnp.float32
        )
        denominator = (
            counts[:, None, None, None]
            * own_means.T[:, :, None, None]
            * jnp.transpose(block_means, (2, 0, 1))[:, None, :, :]
        )
        return (gram_tiles / denominator).reshape(
            local_cycles, frame_rows, blocks.shape[0] * frame_rows
        )

    filled = jnp.zeros((local_cycles, frame_rows, slot_total * frame_rows), jnp.float32)
    filled = lax.dynamic_update_slice(filled, make_tiles(own_block[None]), (0, 0, 0))

    def advance(offset, carry):
        moving, result = carry
        moving = from_behind(moving, "tm", -1)
        result = lax.dynamic_update_slice(
            result, make_tiles(moving[None]), (0, 0, offset * frame_rows)
        )
        return (moving, result)

    _, filled = lax.fori_loop(1, slot_total, advance, (own_block, filled))
    return filled


VMEM = pl.BlockSpec(memory_space=pltpu.VMEM)
HBM = pl.BlockSpec(memory_space=pltpu.HBM)
ANY = pl.BlockSpec(memory_space=pl.ANY)


def local_call(body, outs, count_in, scratch=(), in_specs=None, out_specs=None, after=(), cost=1, **options):
    def ordered(*refs):
        body(*refs[: len(refs) - skipped], *refs[len(refs) - tail :])

    tail = len(outs) + len(scratch)
    skipped = tail + len(after)
    call = pl.pallas_call(
        ordered,
        out_shape=outs,
        in_specs=(in_specs or [VMEM] * count_in) + [ANY] * len(after),
        out_specs=out_specs or [VMEM] * len(outs),
        scratch_shapes=list(scratch),
        compiler_params=pltpu.CompilerParams(vmem_limit_bytes=VMEM_LIMIT),
        cost_estimate=pl.CostEstimate(flops=1, bytes_accessed=cost, transcendentals=0),
        **options,
    )
    return lambda *operands: call(*operands, *after)


def lanes_at(start, width):
    return pl.ds(pl.multiple_of(start, LANES), width)


def owned_kernel(pairs, frames, labels, *outs):
    p = lax.axis_index("pix")
    for k, out in zip((0, 2), outs):
        for n in range(pairs):
            index = (p ^ k) * pairs + n
            live = jnp.where(labels[pl.ds(index, 1), :] >= 0, 1.0, 0.0).astype(jnp.bfloat16)
            out[:, n * LANES : (n + 1) * LANES] = frames[:, lanes_at(index * LANES, LANES)] * live


def near_kernel(loop, per, parts, mine, over, frames, labels, core, *outs):
    to_chip, (*to_time, core_over) = outs[: len(parts)], outs[len(parts) :]
    t = lax.axis_index("tm")
    owned_kernel(loop * per, frames, labels, core, core_over)
    for (start, count), out in zip(parts, to_chip):
        for c in range(loop):
            source = slice((c * per + start) * LANES, (c * per + start + count) * LANES)
            target = slice(c * count * LANES, (c + 1) * count * LANES)
            out[0, :, target] = over[:, source]
            out[1, :, target] = core_over[:, source]
    for j, out in enumerate(to_time, 1):
        lanes = lanes_at((t ^ j) * per * LANES, per * LANES)
        out[0] = mine[:, lanes]
        out[1] = core[:, lanes]


def far_kernel(count, chip, *outs):
    t = lax.axis_index("tm")
    for j, out in enumerate(outs, 1):
        out[...] = chip[:, :, lanes_at((t ^ j) * count * LANES, count * LANES)]


def padded(value):
    wide = value.astype(jnp.float32)
    live = jnp.where(wide[0:1, :] != 0, 1.0, 0.0)
    return jnp.concatenate([wide, jnp.broadcast_to(live, (8, LANES))], axis=0)


def halves(block):
    lane = lax.broadcasted_iota(jnp.int32, block.shape, 1) % LANES
    zero = jnp.zeros_like(block)
    return jnp.concatenate(
        [jnp.where(lane < CYCLE_CAP, block, zero), jnp.where(lane < CYCLE_CAP, zero, block)], axis=0
    )


def normalized(product, rows):
    result = []
    for half in range(2):
        cycle = product[half * (rows + 8) : (half + 1) * (rows + 8)]
        count = cycle[rows : rows + 1, rows : rows + 1]
        row_scale = count / cycle[:rows, rows : rows + 1]
        column_scale = 1.0 / cycle[rows : rows + 1, :]
        result.append(cycle[:rows] * row_scale * column_scale)
    return result


def dot_rows(left, right):
    return lax.dot_general(
        left, right, (((1,), (1,)), ((), ())), preferred_element_type=jnp.float32
    )


def lane_of(rows):
    return lax.broadcasted_iota(jnp.int32, (rows, LANES), 1)


def ordered(refs, order):
    return [refs[order.index(j)] for j in range(1, len(order) + 1)]


def cross_kernel(loop, per, part, rows, last, mine, core, chip, *refs):
    start, count = part
    near, far = ordered(refs[: loop - 1], NEAR), ordered(refs[loop - 1 : 2 * loop - 2], FAR)
    early, outs, blocks = refs[2 * loop - 2 : -1 - loop], refs[-1 - loop : -1], refs[-1]
    t = lax.axis_index("tm")
    lane = lane_of(rows)
    for s in range(count):
        at = lanes_at((t * per + start + s) * LANES, LANES)
        at_near = slice((start + s) * LANES, (start + s + 1) * LANES)
        at_far = slice(s * LANES, (s + 1) * LANES)
        at_chip = lanes_at((t * count + s) * LANES, LANES)
        for j in range(loop):
            if j == 0:
                values = mine[:, at], core[:, at], chip[0, :, at_chip], chip[1, :, at_chip]
            else:
                values = [near[j - 1][k, :, at_near] for k in range(2)] + [far[j - 1][k, :, at_far] for k in range(2)]
            for k, value in enumerate(values):
                blocks[s, t ^ j, :, k * LANES : (k + 1) * LANES] = padded(value).astype(jnp.bfloat16)
    products = {}
    for i in range(loop):
        r = t ^ i
        for s in range(count):
            left = halves(blocks[s, r].astype(jnp.float32)).astype(jnp.bfloat16)
            right = jnp.concatenate(
                [blocks[s, (r + 1) % loop], blocks[s, (r + 2) % loop]], axis=0
            )
            products[i, s] = dot_rows(left, right)
    for i, out in enumerate(outs):
        new = []
        for s in range(count):
            for tile in normalized(products[i, s], rows):
                tile = tile - 1.0
                new.append(jnp.where(lane < rows, tile, pltpu.roll(tile, LANES + rows - CYCLE_CAP, 1)))
        before = [tiles[c] for tiles in early[i::loop] for c in range(tiles.shape[0])]
        if last and i:
            spare = new.pop()
            for m, tile in enumerate(before + new):
                out[m] = jnp.where(lane < 2 * rows, tile, pltpu.roll(spare, (2 * rows - PIECE * m) % LANES, 1))
        else:
            for c, tile in enumerate(before + new):
                out[c] = tile


def own_kernel(loop, per, parts, rows, mine, core, *refs):
    chips, out = refs[:-1], refs[-1]
    for c in range(loop):
        for (start, count), chip in zip(parts, chips):
            for s in range(count):
                n = c * per + start + s
                at = slice(n * LANES, (n + 1) * LANES)
                at_chip = slice((c * count + s) * LANES, (c * count + s + 1) * LANES)
                values = mine[:, at], core[:, at], chip[0, :, at_chip], chip[1, :, at_chip]
                block = jnp.concatenate([padded(value) for value in values], axis=1)
                left = halves(block).astype(jnp.bfloat16)
                block = block.astype(jnp.bfloat16)
                right = jnp.concatenate([block, block], axis=0)
                for half, cycle in enumerate(normalized(dot_rows(left, right), rows)):
                    out[2 * n + half] = cycle


def place_kernel(rows, cycles, partners, own, *refs):
    tiles, (out, slots, sems) = refs[: len(partners)], refs[-3:]
    t = lax.axis_index("tm")
    lane = lane_of(rows)
    copies = []
    for n, (i, part) in enumerate(zip(partners, tiles)):
        at = (t ^ i) * cycles
        for c in range(cycles):
            if c < part.shape[0]:
                value = part[c]
            else:
                value = jnp.zeros((rows, LANES), jnp.float32)
                for m in range(c):
                    piece = pltpu.roll(part[m], PIECE * (m + 1) % LANES, 1)
                    value = jnp.where(lane // PIECE == m, piece, value)
            value = pltpu.roll(value + 1.0, rows, 1)
            slots[n, c, :, :LANES] = jnp.where(lane < rows, own[at + c], value)
            slots[n, c, :, LANES:] = value[:, : 3 * rows - LANES]
        copies.append(pltpu.make_async_copy(slots.at[n], out.at[pl.ds(at, cycles)], sems.at[n]))
        copies[-1].start()
    for copy in copies:
        copy.wait()


def spread(frames, labels, counts):
    loop, groups = lax.axis_size("tm"), lax.axis_size("pix")
    rows = frames.shape[0]
    per = frames.shape[1] // (LANES * groups * loop)
    cycles = 2 * per
    bf16, f32 = jnp.bfloat16, jnp.float32
    parts = [(sum(counts[:n]), count) for n, count in enumerate(counts)]

    def shape(*dims, dtype=bf16):
        return jax.ShapeDtypeStruct(dims, dtype)

    def tiles(count):
        return shape(count, rows, LANES, dtype=f32)

    span = loop * per * LANES
    rows_of_labels = labels.reshape(-1, LANES)
    other = swap(frames, "pix", 1), swap(rows_of_labels, "pix", 1)
    mine, over = local_call(
        functools.partial(owned_kernel, loop * per), [shape(rows, span)] * 2, 2
    )(frames, rows_of_labels)
    core, *ready = local_call(
        functools.partial(near_kernel, loop, per, parts),
        [shape(rows, span)]
        + [shape(2, rows, loop * count * LANES) for _, count in parts]
        + [shape(2, rows, per * LANES)] * (loop - 1),
        4,
        [pltpu.VMEM((rows, span), bf16)],
    )(mine, over, *other)
    chips = [swap(part, "pix", 2) for part in ready[: len(parts)]]
    near = [swap(part, "tm", j) for j, part in enumerate(ready[len(parts) :], 1)]
    early = []
    for part, chip in zip(parts, chips):
        far = local_call(
            functools.partial(far_kernel, part[1]), [shape(2, rows, part[1] * LANES)] * (loop - 1), 1
        )(chip)
        far = [swap(value, "tm", j) for j, value in enumerate(far, 1)]
        last = part is parts[-1]
        early += local_call(
            functools.partial(cross_kernel, loop, per, part, rows, last),
            [tiles(cycles)] + [tiles(cycles - 1)] * (loop - 1) if last else [tiles(2 * part[1])] * loop,
            2 * loop + 1 + (len(early) if last else 0),
            [pltpu.VMEM((part[1], loop, rows + 8, groups * LANES), bf16)],
        )(mine, core, chip, *[near[j - 1] for j in NEAR], *[far[j - 1] for j in FAR], *(early if last else ()))
    kept, *sent = early[-loop:]
    own_tiles = local_call(
        functools.partial(own_kernel, loop, per, parts, rows),
        [tiles(loop * cycles)],
        2 + len(parts),
        cost=OWN_COST,
    )(mine, core, *chips)[0]
    sent = lax.optimization_barrier([part.astype(jnp.float16) for part in sent])
    back = [lax.optimization_barrier(swap(part, "tm", j)) for j, part in enumerate(sent, 1)]
    one, two, three = [part.astype(f32) for part in back]

    def place(partners, parts, *filled):
        return local_call(
            functools.partial(place_kernel, rows, cycles, partners),
            [shape(loop * cycles, rows, 3 * rows, dtype=f32)],
            1 + len(parts) + len(filled),
            [
                pltpu.VMEM((len(partners), cycles, rows, 3 * rows), f32),
                pltpu.SemaphoreType.DMA((len(partners),)),
            ],
            in_specs=[VMEM] * (1 + len(parts)) + [HBM] * len(filled),
            out_specs=[HBM],
            input_output_aliases={1 + len(parts): 0} if filled else {},
            cost=PLACE_COST,
        )(own_tiles, *parts, *filled)[0]

    return place((2, 1), (two, one), place((0, 3), (kept, three)))


def on_device(frames, labels):
    loop, groups = lax.axis_size("tm"), lax.axis_size("pix")
    pairs = CYCLES // groups // 2
    fits = frames.shape[1] == CYCLES * CYCLE_CAP and frames.shape[0] == CYCLE_CAP - 8
    if loop == 4 and groups == 4 and fits and pairs // loop == 4 and pairs % loop == 0:
        return spread(frames, labels, (2, 2))
    return ring(frames, labels)


def solution(mesh):
    placed = (P(("runs", "tm"), "pix"), P("pix"))
    return jax.shard_map(
        on_device,
        mesh=mesh,
        in_specs=placed,
        out_specs=P(("runs", "pix"), "tm", None),
        check_vma=False,
    )
```

```python
import functools

import jax
import jax.numpy as jnp
from jax import lax
from jax.experimental import pallas as pl
from jax.experimental.pallas import tpu as pltpu
from jax.sharding import PartitionSpec as P

CYCLES = 128
CYCLE_CAP = 64
LANES = 128
PIECE = 16
NEAR, FAR = (3, 2, 1), (2, 3, 1)
VMEM_LIMIT = 48 * 2**20
OWN_COST, PLACE_COST = 4 << 20, 4 << 20


def from_behind(shard, axis, by):
    size = lax.axis_size(axis)
    return lax.ppermute(shard, axis, [(i, (i + by) % size) for i in range(size)])


def swap(shard, axis, by):
    size = lax.axis_size(axis)
    return lax.ppermute(shard, axis, [(i, i ^ by) for i in range(size)])


def ring(frames, labels):
    groups = lax.axis_size("pix")
    loop_size = lax.axis_size("tm")
    local_cycles = CYCLES // groups
    slot_total = loop_size // 2 + 1
    frame_rows = frames.shape[0]
    live_row = (labels >= 0).astype(jnp.bfloat16)[None, :]
    masked = frames * live_row
    own_block, live_owned = (
        lax.all_to_all(masked, "pix", split_axis=1, concat_axis=1, tiled=True),
        lax.all_to_all(live_row, "pix", split_axis=1, concat_axis=1, tiled=True),
    )

    def split_cycles(values):
        return values.reshape(values.shape[:-1] + (groups, local_cycles, CYCLE_CAP))

    counts = jnp.sum(split_cycles(live_owned).astype(jnp.float32), axis=(0, 1, 3))
    own_split = split_cycles(own_block)
    own_means = jnp.sum(own_split, axis=(1, 3), dtype=jnp.float32) / counts

    def make_tiles(blocks):
        block_split = split_cycles(blocks)
        block_means = jnp.sum(block_split, axis=(2, 4), dtype=jnp.float32) / counts
        gram_tiles = jnp.einsum(
            "tgqc,nsgqc->qtns", own_split, block_split, preferred_element_type=jnp.float32
        )
        denominator = (
            counts[:, None, None, None]
            * own_means.T[:, :, None, None]
            * jnp.transpose(block_means, (2, 0, 1))[:, None, :, :]
        )
        return (gram_tiles / denominator).reshape(
            local_cycles, frame_rows, blocks.shape[0] * frame_rows
        )

    filled = jnp.zeros((local_cycles, frame_rows, slot_total * frame_rows), jnp.float32)
    filled = lax.dynamic_update_slice(filled, make_tiles(own_block[None]), (0, 0, 0))

    def advance(offset, carry):
        moving, result = carry
        moving = from_behind(moving, "tm", -1)
        result = lax.dynamic_update_slice(
            result, make_tiles(moving[None]), (0, 0, offset * frame_rows)
        )
        return (moving, result)

    _, filled = lax.fori_loop(1, slot_total, advance, (own_block, filled))
    return filled


VMEM = pl.BlockSpec(memory_space=pltpu.VMEM)
HBM = pl.BlockSpec(memory_space=pltpu.HBM)
ANY = pl.BlockSpec(memory_space=pl.ANY)


def local_call(body, outs, count_in, scratch=(), in_specs=None, out_specs=None, after=(), cost=1, **options):
    def ordered(*refs):
        body(*refs[: len(refs) - skipped], *refs[len(refs) - tail :])

    tail = len(outs) + len(scratch)
    skipped = tail + len(after)
    call = pl.pallas_call(
        ordered,
        out_shape=outs,
        in_specs=(in_specs or [VMEM] * count_in) + [ANY] * len(after),
        out_specs=out_specs or [VMEM] * len(outs),
        scratch_shapes=list(scratch),
        compiler_params=pltpu.CompilerParams(vmem_limit_bytes=VMEM_LIMIT),
        cost_estimate=pl.CostEstimate(flops=1, bytes_accessed=cost, transcendentals=0),
        **options,
    )
    return lambda *operands: call(*operands, *after)


def lanes_at(start, width):
    return pl.ds(pl.multiple_of(start, LANES), width)


def owned_kernel(pairs, frames, labels, *outs):
    p = lax.axis_index("pix")
    for k, out in zip((0, 2), outs):
        for n in range(pairs):
            index = (p ^ k) * pairs + n
            live = jnp.where(labels[pl.ds(index, 1), :] >= 0, 1.0, 0.0).astype(jnp.bfloat16)
            out[:, n * LANES : (n + 1) * LANES] = frames[:, lanes_at(index * LANES, LANES)] * live


def near_kernel(loop, per, parts, mine, over, frames, labels, core, *outs):
    to_chip, (*to_time, core_over) = outs[: len(parts)], outs[len(parts) :]
    t = lax.axis_index("tm")
    owned_kernel(loop * per, frames, labels, core, core_over)
    for (start, count), out in zip(parts, to_chip):
        for c in range(loop):
            source = slice((c * per + start) * LANES, (c * per + start + count) * LANES)
            target = slice(c * count * LANES, (c + 1) * count * LANES)
            out[0, :, target] = over[:, source]
            out[1, :, target] = core_over[:, source]
    for j, out in enumerate(to_time, 1):
        lanes = lanes_at((t ^ j) * per * LANES, per * LANES)
        out[0] = mine[:, lanes]
        out[1] = core[:, lanes]


def far_kernel(count, chip, *outs):
    t = lax.axis_index("tm")
    for j, out in enumerate(outs, 1):
        out[...] = chip[:, :, lanes_at((t ^ j) * count * LANES, count * LANES)]


def padded(value):
    wide = value.astype(jnp.float32)
    live = jnp.where(wide[0:1, :] != 0, 1.0, 0.0)
    return jnp.concatenate([wide, jnp.broadcast_to(live, (8, LANES))], axis=0)


def halves(block):
    lane = lax.broadcasted_iota(jnp.int32, block.shape, 1) % LANES
    zero = jnp.zeros_like(block)
    return jnp.concatenate(
        [jnp.where(lane < CYCLE_CAP, block, zero), jnp.where(lane < CYCLE_CAP, zero, block)], axis=0
    )


def normalized(product, rows):
    result = []
    for half in range(2):
        cycle = product[half * (rows + 8) : (half + 1) * (rows + 8)]
        count = cycle[rows : rows + 1, rows : rows + 1]
        row_scale = count / cycle[:rows, rows : rows + 1]
        column_scale = 1.0 / cycle[rows : rows + 1, :]
        result.append(cycle[:rows] * row_scale * column_scale)
    return result


def dot_rows(left, right):
    return lax.dot_general(
        left, right, (((1,), (1,)), ((), ())), preferred_element_type=jnp.float32
    )


def lane_of(rows):
    return lax.broadcasted_iota(jnp.int32, (rows, LANES), 1)


def ordered(refs, order):
    return [refs[order.index(j)] for j in range(1, len(order) + 1)]


def products_of(loop, count, value, blocks, total=None):
    t = lax.axis_index("tm")
    for s in range(count):
        for j in range(loop):
            for k in range(2):
                blocks[s, t ^ j, :, k * LANES : (k + 1) * LANES] = padded(value(s, j, k)).astype(jnp.bfloat16)
    products = {}
    for i in range(loop):
        r = t ^ i
        for s in range(count):
            left = halves(blocks[s, r].astype(jnp.float32)).astype(jnp.bfloat16)
            right = jnp.concatenate(
                [blocks[s, (r + 1) % loop], blocks[s, (r + 2) % loop]], axis=0
            )
            product = dot_rows(left, right)
            products[i, s] = product if total is None else total[i, s] + product
    return products


def near_products_kernel(loop, per, part, mine, core, *refs):
    near, (out, blocks) = ordered(refs[: loop - 1], NEAR), refs[-2:]
    start, count = part
    t = lax.axis_index("tm")

    def value(s, j, k):
        if j:
            return near[j - 1][k, :, (start + s) * LANES : (start + s + 1) * LANES]
        return (mine, core)[k][:, lanes_at((t * per + start + s) * LANES, LANES)]

    for at, product in products_of(loop, count, value, blocks).items():
        out[at] = product


def cross_kernel(loop, part, rows, last, total, chip, *refs):
    far = ordered(refs[: loop - 1], FAR)
    early, outs, blocks = refs[loop - 1 : -1 - loop], refs[-1 - loop : -1], refs[-1]
    count = part[1]
    t = lax.axis_index("tm")
    lane = lane_of(rows)

    def value(s, j, k):
        if j:
            return far[j - 1][k, :, s * LANES : (s + 1) * LANES]
        return chip[k, :, lanes_at((t * count + s) * LANES, LANES)]

    products = products_of(loop, count, value, blocks, total)
    for i, out in enumerate(outs):
        new = []
        for s in range(count):
            for tile in normalized(products[i, s], rows):
                tile = tile - 1.0
                new.append(jnp.where(lane < rows, tile, pltpu.roll(tile, LANES + rows - CYCLE_CAP, 1)))
        before = [tiles[c] for tiles in early[i::loop] for c in range(tiles.shape[0])]
        if last and i:
            spare = new.pop()
            for m, tile in enumerate(before + new):
                out[m] = jnp.where(lane < 2 * rows, tile, pltpu.roll(spare, (2 * rows - PIECE * m) % LANES, 1))
        else:
            for c, tile in enumerate(before + new):
                out[c] = tile


def own_kernel(loop, per, parts, rows, mine, core, *refs):
    chips, out = refs[:-1], refs[-1]
    for c in range(loop):
        for (start, count), chip in zip(parts, chips):
            for s in range(count):
                n = c * per + start + s
                at = slice(n * LANES, (n + 1) * LANES)
                at_chip = slice((c * count + s) * LANES, (c * count + s + 1) * LANES)
                values = mine[:, at], core[:, at], chip[0, :, at_chip], chip[1, :, at_chip]
                block = jnp.concatenate([padded(value) for value in values], axis=1)
                left = halves(block).astype(jnp.bfloat16)
                block = block.astype(jnp.bfloat16)
                right = jnp.concatenate([block, block], axis=0)
                for half, cycle in enumerate(normalized(dot_rows(left, right), rows)):
                    out[2 * n + half] = cycle


def place_kernel(rows, cycles, partners, own, *refs):
    tiles, (out, slots, sems) = refs[: len(partners)], refs[-3:]
    t = lax.axis_index("tm")
    lane = lane_of(rows)
    step = sems.shape[1]
    copies = []
    for n, (i, part) in enumerate(zip(partners, tiles)):
        at = (t ^ i) * cycles
        for c in range(cycles):
            if c < part.shape[0]:
                value = part[c]
            else:
                value = jnp.zeros((rows, LANES), jnp.float32)
                for m in range(c):
                    piece = pltpu.roll(part[m], PIECE * (m + 1) % LANES, 1)
                    value = jnp.where(lane // PIECE == m, piece, value)
            value = pltpu.roll(value + 1.0, rows, 1)
            slots[n, c, :, :LANES] = jnp.where(lane < rows, own[at + c], value)
            slots[n, c, :, LANES:] = value[:, : 3 * rows - LANES]
            if (c + 1) % (cycles // step) == 0:
                size = cycles // step
                copies.append(
                    pltpu.make_async_copy(
                        slots.at[n, pl.ds(c + 1 - size, size)],
                        out.at[pl.ds(at + c + 1 - size, size)],
                        sems.at[n, c // size],
                    )
                )
                copies[-1].start()
    for copy in copies:
        copy.wait()


def spread(frames, labels, counts):
    loop, groups = lax.axis_size("tm"), lax.axis_size("pix")
    rows = frames.shape[0]
    per = frames.shape[1] // (LANES * groups * loop)
    cycles = 2 * per
    bf16, f32 = jnp.bfloat16, jnp.float32
    parts = [(sum(counts[:n]), count) for n, count in enumerate(counts)]

    def shape(*dims, dtype=bf16):
        return jax.ShapeDtypeStruct(dims, dtype)

    def tiles(count):
        return shape(count, rows, LANES, dtype=f32)

    span = loop * per * LANES
    rows_of_labels = labels.reshape(-1, LANES)
    other = swap(frames, "pix", 1), swap(rows_of_labels, "pix", 1)
    mine, over = local_call(
        functools.partial(owned_kernel, loop * per), [shape(rows, span)] * 2, 2
    )(frames, rows_of_labels)
    core, *ready = local_call(
        functools.partial(near_kernel, loop, per, parts),
        [shape(rows, span)]
        + [shape(2, rows, loop * count * LANES) for _, count in parts]
        + [shape(2, rows, per * LANES)] * (loop - 1),
        4,
        [pltpu.VMEM((rows, span), bf16)],
    )(mine, over, *other)
    chips = [swap(part, "pix", 2) for part in ready[: len(parts)]]
    near = [swap(part, "tm", j) for j, part in enumerate(ready[len(parts) :], 1)]
    early = []
    for part, chip in zip(parts, chips):
        far = local_call(
            functools.partial(far_kernel, part[1]), [shape(2, rows, part[1] * LANES)] * (loop - 1), 1
        )(chip)
        far = [swap(value, "tm", j) for j, value in enumerate(far, 1)]
        last = part is parts[-1]
        blocks = pltpu.VMEM((part[1], loop, rows + 8, 2 * LANES), bf16)
        total = local_call(
            functools.partial(near_products_kernel, loop, per, part),
            [shape(loop, part[1], 2 * (rows + 8), LANES, dtype=f32)],
            loop + 1,
            [blocks],
        )(mine, core, *[near[j - 1] for j in NEAR])[0]
        early += local_call(
            functools.partial(cross_kernel, loop, part, rows, last),
            [tiles(cycles)] + [tiles(cycles - 1)] * (loop - 1) if last else [tiles(2 * part[1])] * loop,
            loop + 1 + (len(early) if last else 0),
            [blocks],
        )(total, chip, *[far[j - 1] for j in FAR], *(early if last else ()))
    kept, *sent = early[-loop:]
    own_tiles = local_call(
        functools.partial(own_kernel, loop, per, parts, rows),
        [tiles(loop * cycles)],
        2 + len(parts),
        cost=OWN_COST,
    )(mine, core, *chips)[0]
    sent = lax.optimization_barrier([part.astype(jnp.float16) for part in sent])
    back = [lax.optimization_barrier(swap(part, "tm", j)) for j, part in enumerate(sent, 1)]
    one, two, three = [part.astype(f32) for part in back]

    def place(partners, parts, *filled):
        return local_call(
            functools.partial(place_kernel, rows, cycles, partners),
            [shape(loop * cycles, rows, 3 * rows, dtype=f32)],
            1 + len(parts) + len(filled),
            [
                pltpu.VMEM((len(partners), cycles, rows, 3 * rows), f32),
                pltpu.SemaphoreType.DMA((len(partners), 4)),
            ],
            in_specs=[VMEM] * (1 + len(parts)) + [HBM] * len(filled),
            out_specs=[HBM],
            input_output_aliases={1 + len(parts): 0} if filled else {},
            cost=PLACE_COST,
        )(own_tiles, *parts, *filled)[0]

    return place((2, 1), (two, one), place((0, 3), (kept, three)))


def on_device(frames, labels):
    loop, groups = lax.axis_size("tm"), lax.axis_size("pix")
    pairs = CYCLES // groups // 2
    fits = frames.shape[1] == CYCLES * CYCLE_CAP and frames.shape[0] == CYCLE_CAP - 8
    if loop == 4 and groups == 4 and fits and pairs // loop == 4 and pairs % loop == 0:
        return spread(frames, labels, (2, 2))
    return ring(frames, labels)


def solution(mesh):
    placed = (P(("runs", "tm"), "pix"), P("pix"))
    return jax.shard_map(
        on_device,
        mesh=mesh,
        in_specs=placed,
        out_specs=P(("runs", "pix"), "tm", None),
        check_vma=False,
    )
```

```python
import functools

import jax
import jax.numpy as jnp
from jax import lax
from jax.experimental import pallas as pl
from jax.experimental.pallas import tpu as pltpu
from jax.sharding import PartitionSpec as P

CYCLES = 128
CYCLE_CAP = 64
LANES = 128
PIECE = 16
NEAR, FAR = (3, 2, 1), (2, 3, 1)
VMEM_LIMIT = 48 * 2**20
OWN_COST, PLACE_COST = 4 << 20, 4 << 20


def from_behind(shard, axis, by):
    size = lax.axis_size(axis)
    return lax.ppermute(shard, axis, [(i, (i + by) % size) for i in range(size)])


def swap(shard, axis, by):
    size = lax.axis_size(axis)
    return lax.ppermute(shard, axis, [(i, i ^ by) for i in range(size)])


def ring(frames, labels):
    groups = lax.axis_size("pix")
    loop_size = lax.axis_size("tm")
    local_cycles = CYCLES // groups
    slot_total = loop_size // 2 + 1
    frame_rows = frames.shape[0]
    live_row = (labels >= 0).astype(jnp.bfloat16)[None, :]
    masked = frames * live_row
    own_block, live_owned = (
        lax.all_to_all(masked, "pix", split_axis=1, concat_axis=1, tiled=True),
        lax.all_to_all(live_row, "pix", split_axis=1, concat_axis=1, tiled=True),
    )

    def split_cycles(values):
        return values.reshape(values.shape[:-1] + (groups, local_cycles, CYCLE_CAP))

    counts = jnp.sum(split_cycles(live_owned).astype(jnp.float32), axis=(0, 1, 3))
    own_split = split_cycles(own_block)
    own_means = jnp.sum(own_split, axis=(1, 3), dtype=jnp.float32) / counts

    def make_tiles(blocks):
        block_split = split_cycles(blocks)
        block_means = jnp.sum(block_split, axis=(2, 4), dtype=jnp.float32) / counts
        gram_tiles = jnp.einsum(
            "tgqc,nsgqc->qtns", own_split, block_split, preferred_element_type=jnp.float32
        )
        denominator = (
            counts[:, None, None, None]
            * own_means.T[:, :, None, None]
            * jnp.transpose(block_means, (2, 0, 1))[:, None, :, :]
        )
        return (gram_tiles / denominator).reshape(
            local_cycles, frame_rows, blocks.shape[0] * frame_rows
        )

    filled = jnp.zeros((local_cycles, frame_rows, slot_total * frame_rows), jnp.float32)
    filled = lax.dynamic_update_slice(filled, make_tiles(own_block[None]), (0, 0, 0))

    def advance(offset, carry):
        moving, result = carry
        moving = from_behind(moving, "tm", -1)
        result = lax.dynamic_update_slice(
            result, make_tiles(moving[None]), (0, 0, offset * frame_rows)
        )
        return (moving, result)

    _, filled = lax.fori_loop(1, slot_total, advance, (own_block, filled))
    return filled


VMEM = pl.BlockSpec(memory_space=pltpu.VMEM)
HBM = pl.BlockSpec(memory_space=pltpu.HBM)
ANY = pl.BlockSpec(memory_space=pl.ANY)


def local_call(body, outs, count_in, scratch=(), in_specs=None, out_specs=None, after=(), cost=1, **options):
    def ordered(*refs):
        body(*refs[: len(refs) - skipped], *refs[len(refs) - tail :])

    tail = len(outs) + len(scratch)
    skipped = tail + len(after)
    call = pl.pallas_call(
        ordered,
        out_shape=outs,
        in_specs=(in_specs or [VMEM] * count_in) + [ANY] * len(after),
        out_specs=out_specs or [VMEM] * len(outs),
        scratch_shapes=list(scratch),
        compiler_params=pltpu.CompilerParams(vmem_limit_bytes=VMEM_LIMIT),
        cost_estimate=pl.CostEstimate(flops=1, bytes_accessed=cost, transcendentals=0),
        **options,
    )
    return lambda *operands: call(*operands, *after)


def lanes_at(start, width):
    return pl.ds(pl.multiple_of(start, LANES), width)


def owned_kernel(pairs, frames, labels, *outs):
    p = lax.axis_index("pix")
    for k, out in zip((0, 2), outs):
        for n in range(pairs):
            index = (p ^ k) * pairs + n
            live = jnp.where(labels[pl.ds(index, 1), :] >= 0, 1.0, 0.0).astype(jnp.bfloat16)
            out[:, n * LANES : (n + 1) * LANES] = frames[:, lanes_at(index * LANES, LANES)] * live


def near_kernel(loop, per, parts, mine, over, frames, labels, core, *outs):
    to_chip, (*to_time, core_over) = outs[: len(parts)], outs[len(parts) :]
    t = lax.axis_index("tm")
    owned_kernel(loop * per, frames, labels, core, core_over)
    for (start, count), out in zip(parts, to_chip):
        for c in range(loop):
            source = slice((c * per + start) * LANES, (c * per + start + count) * LANES)
            target = slice(c * count * LANES, (c + 1) * count * LANES)
            out[0, :, target] = over[:, source]
            out[1, :, target] = core_over[:, source]
    for j, out in enumerate(to_time, 1):
        lanes = lanes_at((t ^ j) * per * LANES, per * LANES)
        out[0] = mine[:, lanes]
        out[1] = core[:, lanes]


def far_kernel(count, chip, *outs):
    t = lax.axis_index("tm")
    for j, out in enumerate(outs, 1):
        out[...] = chip[:, :, lanes_at((t ^ j) * count * LANES, count * LANES)]


def padded(value):
    wide = value.astype(jnp.float32)
    live = jnp.where(wide[0:1, :] != 0, 1.0, 0.0)
    return jnp.concatenate([wide, jnp.broadcast_to(live, (8, LANES))], axis=0)


def halves(block):
    lane = lax.broadcasted_iota(jnp.int32, (1, block.shape[1]), 1) % LANES
    even = jnp.where(lane < CYCLE_CAP, 1.0, 0.0).astype(block.dtype)
    odd = jnp.where(lane < CYCLE_CAP, 0.0, 1.0).astype(block.dtype)
    return jnp.concatenate([block * even, block * odd], axis=0)


def normalized(product, rows):
    result = []
    for half in range(2):
        cycle = product[half * (rows + 8) : (half + 1) * (rows + 8)]
        count = cycle[rows : rows + 1, rows : rows + 1]
        column_scale = count / cycle[rows : rows + 1, :]
        row_scale = 1.0 / cycle[:rows, rows : rows + 1]
        result.append(cycle[:rows] * (row_scale * column_scale))
    return result


def dot_rows(left, right):
    return lax.dot_general(
        left, right, (((1,), (1,)), ((), ())), preferred_element_type=jnp.float32
    )


def lane_of(rows):
    return lax.broadcasted_iota(jnp.int32, (rows, LANES), 1)


def ordered(refs, order):
    return [refs[order.index(j)] for j in range(1, len(order) + 1)]


def products_of(loop, count, value, blocks, total=None):
    t = lax.axis_index("tm")
    for s in range(count):
        for j in range(loop):
            for k in range(2):
                blocks[s, t ^ j, :, k * LANES : (k + 1) * LANES] = padded(value(s, j, k)).astype(jnp.bfloat16)
    products = {}
    for i in range(loop):
        r = t ^ i
        for s in range(count):
            left = halves(blocks[s, r])
            right = jnp.concatenate(
                [blocks[s, (r + 1) % loop], blocks[s, (r + 2) % loop]], axis=0
            )
            product = dot_rows(left, right)
            products[i, s] = product if total is None else total[i, s] + product
    return products


def near_products_kernel(loop, per, part, mine, core, *refs):
    near, (out, blocks) = ordered(refs[: loop - 1], NEAR), refs[-2:]
    start, count = part
    t = lax.axis_index("tm")

    def value(s, j, k):
        if j:
            return near[j - 1][k, :, (start + s) * LANES : (start + s + 1) * LANES]
        return (mine, core)[k][:, lanes_at((t * per + start + s) * LANES, LANES)]

    for at, product in products_of(loop, count, value, blocks).items():
        out[at] = product


def cross_kernel(loop, part, rows, last, total, chip, *refs):
    far = ordered(refs[: loop - 1], FAR)
    early, outs, blocks = refs[loop - 1 : -1 - loop], refs[-1 - loop : -1], refs[-1]
    count = part[1]
    t = lax.axis_index("tm")
    lane = lane_of(rows)

    def value(s, j, k):
        if j:
            return far[j - 1][k, :, s * LANES : (s + 1) * LANES]
        return chip[k, :, lanes_at((t * count + s) * LANES, LANES)]

    products = products_of(loop, count, value, blocks, total)
    for i, out in enumerate(outs):
        new = []
        for s in range(count):
            for tile in normalized(products[i, s], rows):
                tile = tile - 1.0
                new.append(jnp.where(lane < rows, tile, pltpu.roll(tile, LANES + rows - CYCLE_CAP, 1)))
        before = [tiles[c] for tiles in early[i::loop] for c in range(tiles.shape[0])]
        if last and i:
            spare = new.pop()
            for m, tile in enumerate(before + new):
                out[m] = jnp.where(lane < 2 * rows, tile, pltpu.roll(spare, (2 * rows - PIECE * m) % LANES, 1))
        else:
            for c, tile in enumerate(before + new):
                out[c] = tile


def own_kernel(loop, per, parts, rows, mine, core, *refs):
    chips, out = refs[:-1], refs[-1]
    for c in range(loop):
        for (start, count), chip in zip(parts, chips):
            for s in range(count):
                n = c * per + start + s
                at = slice(n * LANES, (n + 1) * LANES)
                at_chip = slice((c * count + s) * LANES, (c * count + s + 1) * LANES)
                values = mine[:, at], core[:, at], chip[0, :, at_chip], chip[1, :, at_chip]
                block = jnp.concatenate([padded(value) for value in values], axis=1)
                block = block.astype(jnp.bfloat16)
                left = halves(block)
                right = jnp.concatenate([block, block], axis=0)
                for half, cycle in enumerate(normalized(dot_rows(left, right), rows)):
                    out[2 * n + half] = cycle


def place_kernel(rows, cycles, partners, own, *refs):
    tiles, (out, slots, sems) = refs[: len(partners)], refs[-3:]
    t = lax.axis_index("tm")
    lane = lane_of(rows)
    step = sems.shape[1]
    copies = []
    for n, (i, part) in enumerate(zip(partners, tiles)):
        at = (t ^ i) * cycles
        for c in range(cycles):
            if c < part.shape[0]:
                value = part[c]
            else:
                value = jnp.zeros((rows, LANES), jnp.float32)
                for m in range(c):
                    piece = pltpu.roll(part[m], PIECE * (m + 1) % LANES, 1)
                    value = jnp.where(lane // PIECE == m, piece, value)
            value = pltpu.roll(value + 1.0, rows, 1)
            slots[n, c, :, :LANES] = jnp.where(lane < rows, own[at + c], value)
            slots[n, c, :, LANES:] = value[:, : 3 * rows - LANES]
            if (c + 1) % (cycles // step) == 0:
                size = cycles // step
                copies.append(
                    pltpu.make_async_copy(
                        slots.at[n, pl.ds(c + 1 - size, size)],
                        out.at[pl.ds(at + c + 1 - size, size)],
                        sems.at[n, c // size],
                    )
                )
                copies[-1].start()
    for copy in copies:
        copy.wait()


def spread(frames, labels, counts):
    loop, groups = lax.axis_size("tm"), lax.axis_size("pix")
    rows = frames.shape[0]
    per = frames.shape[1] // (LANES * groups * loop)
    cycles = 2 * per
    bf16, f32 = jnp.bfloat16, jnp.float32
    parts = [(sum(counts[:n]), count) for n, count in enumerate(counts)]

    def shape(*dims, dtype=bf16):
        return jax.ShapeDtypeStruct(dims, dtype)

    def tiles(count):
        return shape(count, rows, LANES, dtype=f32)

    span = loop * per * LANES
    rows_of_labels = labels.reshape(-1, LANES)
    other = swap(frames, "pix", 1), swap(rows_of_labels, "pix", 1)
    mine, over = local_call(
        functools.partial(owned_kernel, loop * per), [shape(rows, span)] * 2, 2
    )(frames, rows_of_labels)
    core, *ready = local_call(
        functools.partial(near_kernel, loop, per, parts),
        [shape(rows, span)]
        + [shape(2, rows, loop * count * LANES) for _, count in parts]
        + [shape(2, rows, per * LANES)] * (loop - 1),
        4,
        [pltpu.VMEM((rows, span), bf16)],
    )(mine, over, *other)
    chips = [swap(part, "pix", 2) for part in ready[: len(parts)]]
    near = [swap(part, "tm", j) for j, part in enumerate(ready[len(parts) :], 1)]
    early = []
    for part, chip in zip(parts, chips):
        far = local_call(
            functools.partial(far_kernel, part[1]), [shape(2, rows, part[1] * LANES)] * (loop - 1), 1
        )(chip)
        far = [swap(value, "tm", j) for j, value in enumerate(far, 1)]
        last = part is parts[-1]
        blocks = pltpu.VMEM((part[1], loop, rows + 8, 2 * LANES), bf16)
        total = local_call(
            functools.partial(near_products_kernel, loop, per, part),
            [shape(loop, part[1], 2 * (rows + 8), LANES, dtype=f32)],
            loop + 1,
            [blocks],
        )(mine, core, *[near[j - 1] for j in NEAR])[0]
        early += local_call(
            functools.partial(cross_kernel, loop, part, rows, last),
            [tiles(cycles)] + [tiles(cycles - 1)] * (loop - 1) if last else [tiles(2 * part[1])] * loop,
            loop + 1 + (len(early) if last else 0),
            [blocks],
        )(total, chip, *[far[j - 1] for j in FAR], *(early if last else ()))
    kept, *sent = early[-loop:]
    own_tiles = local_call(
        functools.partial(own_kernel, loop, per, parts, rows),
        [tiles(loop * cycles)],
        2 + len(parts),
        cost=OWN_COST,
    )(mine, core, *chips)[0]
    sent = lax.optimization_barrier([part.astype(jnp.float16) for part in sent])
    back = [lax.optimization_barrier(swap(part, "tm", j)) for j, part in enumerate(sent, 1)]
    one, two, three = [part.astype(f32) for part in back]

    def place(partners, parts, *filled):
        return local_call(
            functools.partial(place_kernel, rows, cycles, partners),
            [shape(loop * cycles, rows, 3 * rows, dtype=f32)],
            1 + len(parts) + len(filled),
            [
                pltpu.VMEM((len(partners), cycles, rows, 3 * rows), f32),
                pltpu.SemaphoreType.DMA((len(partners), 4)),
            ],
            in_specs=[VMEM] * (1 + len(parts)) + [HBM] * len(filled),
            out_specs=[HBM],
            input_output_aliases={1 + len(parts): 0} if filled else {},
            cost=PLACE_COST,
        )(own_tiles, *parts, *filled)[0]

    return place((2, 1), (two, one), place((0, 3), (kept, three)))


def on_device(frames, labels):
    loop, groups = lax.axis_size("tm"), lax.axis_size("pix")
    pairs = CYCLES // groups // 2
    fits = frames.shape[1] == CYCLES * CYCLE_CAP and frames.shape[0] == CYCLE_CAP - 8
    if loop == 4 and groups == 4 and fits and pairs // loop == 4 and pairs % loop == 0:
        return spread(frames, labels, (2, 2))
    return ring(frames, labels)


def solution(mesh):
    placed = (P(("runs", "tm"), "pix"), P("pix"))
    return jax.shard_map(
        on_device,
        mesh=mesh,
        in_specs=placed,
        out_specs=P(("runs", "pix"), "tm", None),
        check_vma=False,
    )
```

```python
import functools

import jax
import jax.numpy as jnp
from jax import lax
from jax.experimental import pallas as pl
from jax.experimental.pallas import tpu as pltpu
from jax.sharding import PartitionSpec as P

CYCLES = 128
CYCLE_CAP = 64
LANES = 128
PIECE = 16
NEAR, FAR = (3, 2, 1), (2, 3, 1)
VMEM_LIMIT = 48 * 2**20
OWN_COST, PLACE_COST = 4 << 20, 4 << 20


def from_behind(shard, axis, by):
    size = lax.axis_size(axis)
    return lax.ppermute(shard, axis, [(i, (i + by) % size) for i in range(size)])


def swap(shard, axis, by):
    size = lax.axis_size(axis)
    return lax.ppermute(shard, axis, [(i, i ^ by) for i in range(size)])


def ring(frames, labels):
    groups = lax.axis_size("pix")
    loop_size = lax.axis_size("tm")
    local_cycles = CYCLES // groups
    slot_total = loop_size // 2 + 1
    frame_rows = frames.shape[0]
    live_row = (labels >= 0).astype(jnp.bfloat16)[None, :]
    masked = frames * live_row
    own_block, live_owned = (
        lax.all_to_all(masked, "pix", split_axis=1, concat_axis=1, tiled=True),
        lax.all_to_all(live_row, "pix", split_axis=1, concat_axis=1, tiled=True),
    )

    def split_cycles(values):
        return values.reshape(values.shape[:-1] + (groups, local_cycles, CYCLE_CAP))

    counts = jnp.sum(split_cycles(live_owned).astype(jnp.float32), axis=(0, 1, 3))
    own_split = split_cycles(own_block)
    own_means = jnp.sum(own_split, axis=(1, 3), dtype=jnp.float32) / counts

    def make_tiles(blocks):
        block_split = split_cycles(blocks)
        block_means = jnp.sum(block_split, axis=(2, 4), dtype=jnp.float32) / counts
        gram_tiles = jnp.einsum(
            "tgqc,nsgqc->qtns", own_split, block_split, preferred_element_type=jnp.float32
        )
        denominator = (
            counts[:, None, None, None]
            * own_means.T[:, :, None, None]
            * jnp.transpose(block_means, (2, 0, 1))[:, None, :, :]
        )
        return (gram_tiles / denominator).reshape(
            local_cycles, frame_rows, blocks.shape[0] * frame_rows
        )

    filled = jnp.zeros((local_cycles, frame_rows, slot_total * frame_rows), jnp.float32)
    filled = lax.dynamic_update_slice(filled, make_tiles(own_block[None]), (0, 0, 0))

    def advance(offset, carry):
        moving, result = carry
        moving = from_behind(moving, "tm", -1)
        result = lax.dynamic_update_slice(
            result, make_tiles(moving[None]), (0, 0, offset * frame_rows)
        )
        return (moving, result)

    _, filled = lax.fori_loop(1, slot_total, advance, (own_block, filled))
    return filled


VMEM = pl.BlockSpec(memory_space=pltpu.VMEM)
HBM = pl.BlockSpec(memory_space=pltpu.HBM)
ANY = pl.BlockSpec(memory_space=pl.ANY)


def local_call(body, outs, count_in, scratch=(), in_specs=None, out_specs=None, after=(), cost=1, **options):
    def ordered(*refs):
        body(*refs[: len(refs) - skipped], *refs[len(refs) - tail :])

    tail = len(outs) + len(scratch)
    skipped = tail + len(after)
    call = pl.pallas_call(
        ordered,
        out_shape=outs,
        in_specs=(in_specs or [VMEM] * count_in) + [ANY] * len(after),
        out_specs=out_specs or [VMEM] * len(outs),
        scratch_shapes=list(scratch),
        compiler_params=pltpu.CompilerParams(vmem_limit_bytes=VMEM_LIMIT),
        cost_estimate=pl.CostEstimate(flops=1, bytes_accessed=cost, transcendentals=0),
        **options,
    )
    return lambda *operands: call(*operands, *after)


def lanes_at(start, width):
    return pl.ds(pl.multiple_of(start, LANES), width)


def owned_kernel(pairs, frames, labels, *outs):
    p = lax.axis_index("pix")
    for k, out in zip((0, 2), outs):
        for n in range(pairs):
            index = (p ^ k) * pairs + n
            live = jnp.where(labels[pl.ds(index, 1), :] >= 0, 1.0, 0.0).astype(jnp.bfloat16)
            out[:, n * LANES : (n + 1) * LANES] = frames[:, lanes_at(index * LANES, LANES)] * live


def near_kernel(loop, per, parts, mine, over, frames, labels, core, *outs):
    to_chip, to_time = outs[: len(parts)], outs[len(parts) :]
    t, p = lax.axis_index("tm"), lax.axis_index("pix")
    owned_kernel(loop * per, frames, labels, core)
    for (start, count), out in zip(parts, to_chip):
        for c in range(loop):
            source = slice((c * per + start) * LANES, (c * per + start + count) * LANES)
            target = slice(c * count * LANES, (c + 1) * count * LANES)
            out[0, :, target] = over[:, source]
            for s in range(count):
                index = ((p ^ 2) * loop + c) * per + start + s
                live = jnp.where(labels[pl.ds(index, 1), :] >= 0, 1.0, 0.0).astype(jnp.bfloat16)
                at = slice((c * count + s) * LANES, (c * count + s + 1) * LANES)
                out[1, :, at] = frames[:, lanes_at(index * LANES, LANES)] * live
    for j, out in enumerate(to_time, 1):
        lanes = lanes_at((t ^ j) * per * LANES, per * LANES)
        out[0] = mine[:, lanes]
        out[1] = core[:, lanes]


def far_kernel(count, chip, *outs):
    t = lax.axis_index("tm")
    for j, out in enumerate(outs, 1):
        out[...] = chip[:, :, lanes_at((t ^ j) * count * LANES, count * LANES)]


def padded(value):
    wide = value.astype(jnp.float32)
    live = jnp.where(wide[0:1, :] != 0, 1.0, 0.0)
    return jnp.concatenate([wide, jnp.broadcast_to(live, (8, LANES))], axis=0)


def halves(block):
    lane = lax.broadcasted_iota(jnp.int32, block.shape, 1) % LANES
    zero = jnp.zeros_like(block)
    return jnp.concatenate(
        [jnp.where(lane < CYCLE_CAP, block, zero), jnp.where(lane < CYCLE_CAP, zero, block)], axis=0
    )


def normalized(product, rows):
    result = []
    for half in range(2):
        cycle = product[half * (rows + 8) : (half + 1) * (rows + 8)]
        count = cycle[rows : rows + 1, rows : rows + 1]
        row_scale = count / cycle[:rows, rows : rows + 1]
        column_scale = 1.0 / cycle[rows : rows + 1, :]
        result.append(cycle[:rows] * row_scale * column_scale)
    return result


def dot_rows(left, right):
    return lax.dot_general(
        left, right, (((1,), (1,)), ((), ())), preferred_element_type=jnp.float32
    )


def lane_of(rows):
    return lax.broadcasted_iota(jnp.int32, (rows, LANES), 1)


def ordered(refs, order):
    return [refs[order.index(j)] for j in range(1, len(order) + 1)]


def products_of(loop, count, value, blocks, total=None):
    t = lax.axis_index("tm")
    for s in range(count):
        for j in range(loop):
            for k in range(2):
                blocks[s, t ^ j, :, k * LANES : (k + 1) * LANES] = padded(value(s, j, k)).astype(jnp.bfloat16)
    products = {}
    for i in range(loop):
        r = t ^ i
        for s in range(count):
            left = halves(blocks[s, r].astype(jnp.float32)).astype(jnp.bfloat16)
            right = jnp.concatenate(
                [blocks[s, (r + 1) % loop], blocks[s, (r + 2) % loop]], axis=0
            )
            product = dot_rows(left, right)
            products[i, s] = product if total is None else total[i, s] + product
    return products


def near_products_kernel(loop, per, part, mine, core, *refs):
    near, (out, blocks) = ordered(refs[: loop - 1], NEAR), refs[-2:]
    start, count = part
    t = lax.axis_index("tm")

    def value(s, j, k):
        if j:
            return near[j - 1][k, :, (start + s) * LANES : (start + s + 1) * LANES]
        return (mine, core)[k][:, lanes_at((t * per + start + s) * LANES, LANES)]

    for at, product in products_of(loop, count, value, blocks).items():
        out[at] = product


def cross_kernel(loop, part, rows, last, total, chip, *refs):
    far = ordered(refs[: loop - 1], FAR)
    early, outs, blocks = refs[loop - 1 : -1 - loop], refs[-1 - loop : -1], refs[-1]
    count = part[1]
    t = lax.axis_index("tm")
    lane = lane_of(rows)

    def value(s, j, k):
        if j:
            return far[j - 1][k, :, s * LANES : (s + 1) * LANES]
        return chip[k, :, lanes_at((t * count + s) * LANES, LANES)]

    products = products_of(loop, count, value, blocks, total)
    for i, out in enumerate(outs):
        new = []
        for s in range(count):
            for tile in normalized(products[i, s], rows):
                tile = tile - 1.0
                new.append(jnp.where(lane < rows, tile, pltpu.roll(tile, LANES + rows - CYCLE_CAP, 1)))
        before = [tiles[c] for tiles in early[i::loop] for c in range(tiles.shape[0])]
        if last and i:
            spare = new.pop()
            for m, tile in enumerate(before + new):
                out[m] = jnp.where(lane < 2 * rows, tile, pltpu.roll(spare, (2 * rows - PIECE * m) % LANES, 1))
        else:
            for c, tile in enumerate(before + new):
                out[c] = tile


def own_kernel(loop, per, parts, rows, mine, core, *refs):
    chips, out = refs[:-1], refs[-1]
    for c in range(loop):
        for (start, count), chip in zip(parts, chips):
            for s in range(count):
                n = c * per + start + s
                at = slice(n * LANES, (n + 1) * LANES)
                at_chip = slice((c * count + s) * LANES, (c * count + s + 1) * LANES)
                values = mine[:, at], core[:, at], chip[0, :, at_chip], chip[1, :, at_chip]
                block = jnp.concatenate([padded(value) for value in values], axis=1)
                left = halves(block).astype(jnp.bfloat16)
                block = block.astype(jnp.bfloat16)
                right = jnp.concatenate([block, block], axis=0)
                for half, cycle in enumerate(normalized(dot_rows(left, right), rows)):
                    out[2 * n + half] = cycle


def place_kernel(rows, cycles, partners, own, *refs):
    tiles, (out, slots, sems) = refs[: len(partners)], refs[-3:]
    t = lax.axis_index("tm")
    lane = lane_of(rows)
    step = sems.shape[1]
    copies = []
    for n, (i, part) in enumerate(zip(partners, tiles)):
        at = (t ^ i) * cycles
        for c in range(cycles):
            if c < part.shape[0]:
                value = part[c]
            else:
                value = jnp.zeros((rows, LANES), jnp.float32)
                for m in range(c):
                    piece = pltpu.roll(part[m], PIECE * (m + 1) % LANES, 1)
                    value = jnp.where(lane // PIECE == m, piece, value)
            value = pltpu.roll(value + 1.0, rows, 1)
            slots[n, c, :, :LANES] = jnp.where(lane < rows, own[at + c], value)
            slots[n, c, :, LANES:] = value[:, : 3 * rows - LANES]
            if (c + 1) % (cycles // step) == 0:
                size = cycles // step
                copies.append(
                    pltpu.make_async_copy(
                        slots.at[n, pl.ds(c + 1 - size, size)],
                        out.at[pl.ds(at + c + 1 - size, size)],
                        sems.at[n, c // size],
                    )
                )
                copies[-1].start()
    for copy in copies:
        copy.wait()


def spread(frames, labels, counts):
    loop, groups = lax.axis_size("tm"), lax.axis_size("pix")
    rows = frames.shape[0]
    per = frames.shape[1] // (LANES * groups * loop)
    cycles = 2 * per
    bf16, f32 = jnp.bfloat16, jnp.float32
    parts = [(sum(counts[:n]), count) for n, count in enumerate(counts)]

    def shape(*dims, dtype=bf16):
        return jax.ShapeDtypeStruct(dims, dtype)

    def tiles(count):
        return shape(count, rows, LANES, dtype=f32)

    span = loop * per * LANES
    rows_of_labels = labels.reshape(-1, LANES)
    other = swap(frames, "pix", 1), swap(rows_of_labels, "pix", 1)
    mine, over = local_call(
        functools.partial(owned_kernel, loop * per), [shape(rows, span)] * 2, 2
    )(frames, rows_of_labels)
    core, *ready = local_call(
        functools.partial(near_kernel, loop, per, parts),
        [shape(rows, span)]
        + [shape(2, rows, loop * count * LANES) for _, count in parts]
        + [shape(2, rows, per * LANES)] * (loop - 1),
        4,
    )(mine, over, *other)
    chips = [swap(part, "pix", 2) for part in ready[: len(parts)]]
    near = [swap(part, "tm", j) for j, part in enumerate(ready[len(parts) :], 1)]
    early = []
    for part, chip in zip(parts, chips):
        far = local_call(
            functools.partial(far_kernel, part[1]), [shape(2, rows, part[1] * LANES)] * (loop - 1), 1
        )(chip)
        far = [swap(value, "tm", j) for j, value in enumerate(far, 1)]
        last = part is parts[-1]
        blocks = pltpu.VMEM((part[1], loop, rows + 8, 2 * LANES), bf16)
        total = local_call(
            functools.partial(near_products_kernel, loop, per, part),
            [shape(loop, part[1], 2 * (rows + 8), LANES, dtype=f32)],
            loop + 1,
            [blocks],
        )(mine, core, *[near[j - 1] for j in NEAR])[0]
        early += local_call(
            functools.partial(cross_kernel, loop, part, rows, last),
            [tiles(cycles)] + [tiles(cycles - 1)] * (loop - 1) if last else [tiles(2 * part[1])] * loop,
            loop + 1 + (len(early) if last else 0),
            [blocks],
        )(total, chip, *[far[j - 1] for j in FAR], *(early if last else ()))
    kept, *sent = early[-loop:]
    own_tiles = local_call(
        functools.partial(own_kernel, loop, per, parts, rows),
        [tiles(loop * cycles)],
        2 + len(parts),
        cost=OWN_COST,
    )(mine, core, *chips)[0]
    sent = lax.optimization_barrier([part.astype(jnp.float16) for part in sent])
    back = [lax.optimization_barrier(swap(part, "tm", j)) for j, part in enumerate(sent, 1)]
    one, two, three = [part.astype(f32) for part in back]

    def place(partners, parts, *filled):
        return local_call(
            functools.partial(place_kernel, rows, cycles, partners),
            [shape(loop * cycles, rows, 3 * rows, dtype=f32)],
            1 + len(parts) + len(filled),
            [
                pltpu.VMEM((len(partners), cycles, rows, 3 * rows), f32),
                pltpu.SemaphoreType.DMA((len(partners), 4)),
            ],
            in_specs=[VMEM] * (1 + len(parts)) + [HBM] * len(filled),
            out_specs=[HBM],
            input_output_aliases={1 + len(parts): 0} if filled else {},
            cost=PLACE_COST,
        )(own_tiles, *parts, *filled)[0]

    return place((2, 1), (two, one), place((0, 3), (kept, three)))


def on_device(frames, labels):
    loop, groups = lax.axis_size("tm"), lax.axis_size("pix")
    pairs = CYCLES // groups // 2
    fits = frames.shape[1] == CYCLES * CYCLE_CAP and frames.shape[0] == CYCLE_CAP - 8
    if loop == 4 and groups == 4 and fits and pairs // loop == 4 and pairs % loop == 0:
        return spread(frames, labels, (2, 2))
    return ring(frames, labels)


def solution(mesh):
    placed = (P(("runs", "tm"), "pix"), P("pix"))
    return jax.shard_map(
        on_device,
        mesh=mesh,
        in_specs=placed,
        out_specs=P(("runs", "pix"), "tm", None),
        check_vma=False,
    )
```
